32 devices in a mesh: dp: 2 (over x), ctx: 4 (over y, core), tp: 4 (over z).
Axes of the slice: x: 2, y: 2, z: 4, core: 2. Of those that a mesh axis runs over, the one named last changes fastest.
Arguments:
- tokens: bfloat16 [2, 4096, 2048], P('dp', ('ctx', 'tp')), may hold values from -6 to 6
- lengths: int32 [2, 8], P('dp'), may hold values from 1 to 3584, 4096 in all within a row
- q_weight: bfloat16 [2048, 2048], P(None, 'tp'), may hold values from -0.1875 to 0.1875
- k_weight: bfloat16 [2048, 512], P(None, 'tp'), may hold values from -0.1875 to 0.1875
- v_weight: bfloat16 [2048, 512], P(None, 'tp'), may hold values from -0.125 to 0.125
- o_weight: bfloat16 [2048, 2048], P('tp'), may hold values from -1 to 1
- gate_weight: bfloat16 [2048, 8192], P(None, 'tp'), may hold values from -0.125 to 0.125
- up_weight: bfloat16 [2048, 8192], P(None, 'tp'), may hold values from -0.125 to 0.125
- down_weight: bfloat16 [8192, 2048], P('tp'), may hold values from -0.0625 to 0.0625
- attention_norm_gain: float32 [2048], replicated, may hold values from 0.5 to 1.5
- feedforward_norm_gain: float32 [2048], replicated, may hold values from 0.5 to 1.5
- cotangent: bfloat16 [2, 4096, 2048], P('dp', ('ctx', 'tp')), may hold values from -6 to 6
Outputs:
- output: bfloat16 [2, 4096, 2048], P('dp', ('ctx', 'tp'))
- input_token_gradient: bfloat16 [2, 4096, 2048], P('dp', ('ctx', 'tp'))
- d_q_weight: float32 [2048, 2048], P(None, 'tp')
- d_k_weight: float32 [2048, 512], P(None, 'tp')
- d_v_weight: float32 [2048, 512], P(None, 'tp')
- d_o_weight: float32 [2048, 2048], P('tp')
- d_gate_weight: float32 [2048, 8192], P(None, 'tp')
- d_up_weight: float32 [2048, 8192], P(None, 'tp')
- d_down_weight: float32 [8192, 2048], P('tp')
- d_attn_gain: float32 [2048], replicated
- d_ffn_gain: float32 [2048], replicated
The draws below stay inside these ranges and needn't reach their ends.
Inputs may be any that keep to these rules, and one draw needn't show every extreme that they name: Each row's 8 lengths sum to 4096.
All inputs are finite; a program needn't handle non-finite values.
Results may differ from the reference program's by a relative error of at most 0.025.
Values may be sent and summed in bfloat16 or wider, within the bound.
No kernel may reach another device: no remote copies, remote signals or barrier semaphores. Data moves between devices by JAX's collectives and lax.ppermute only.
A program may use at most 320 MiB of HBM per device.

```python
import math
import jax
import jax.numpy as jnp
import numpy as np
from jax import lax

D = 2048
HEADS = 32
KV_HEADS = 8
HEAD = 64
FF = 8192
TOK_CTX = 1024
NDOC = 8
SEQ = 4096
ROWS = 2


def levels(own_key, extent, shards, least, high):
    gain, own = 1.0, jax.random.fold_in(own_key, 6)
    for axis_at, parts in shards:
        draws = jnp.exp(jax.random.uniform(jax.random.fold_in(own, axis_at), (parts,), jnp.float32, least / len(shards), high / len(shards)))
        gain = gain * jnp.repeat(draws, extent[axis_at] // parts).reshape([-1 if axis == axis_at else 1 for axis in range(len(extent))])
    return gain


def length_profile(amount, total, most, lean):
    weights = [(1 << 20) // math.isqrt(standing ** lean) + 1 for standing in range(2, amount + 1)]
    rest, holding = total - most - (amount - 1), [1] * (amount - 1)
    while rest > 0:
        movable = [i for i in range(amount - 1) if holding[i] < most]
        whole, budget = sum([weights[i] for i in movable]), rest
        for i in movable:
            extra = min(most - holding[i], max(1, budget * weights[i] // whole), rest)
            holding[i] = holding[i] + extra
            rest = rest - extra
    return np.array([most] + holding)


def uneven_parts(own_key, amount, total, limit, slope):
    if amount == 2:
        one = jax.random.randint(own_key, (), max(1, total - limit), min(limit, total - 1) + 1)
        return jnp.stack([one, total - one])
    sizes = jnp.asarray(length_profile(amount, total, limit, slope), jnp.int32)
    twos = (amount - 1) // 2
    giver, taker = sizes[1:1 + 2 * twos:2], sizes[2:2 + 2 * twos:2]
    slack = jnp.minimum(giver - 1, limit - taker)
    shifted = jax.random.randint(jax.random.fold_in(own_key, 1), (twos,), 0, 1 << 20) % (slack + 1)
    sizes = sizes.at[1:1 + 2 * twos:2].set(giver - shifted).at[2:2 + 2 * twos:2].set(taker + shifted)
    return sizes[jax.random.permutation(jax.random.fold_in(own_key, 2), amount)]


def scatter_about(rng, dims, width, most, shards=(), kind=jnp.bfloat16):
    array = jax.random.normal(rng, dims, jnp.float32) * width
    if len(shards) > 0:
        array = levels(rng, dims, shards, -0.22, 0.18) * array
    return jnp.clip(array, min=-most, max=most).astype(kind)


def setup_inputs(seed: int = 0) -> dict:
    key_list = jax.random.split(jax.random.key(seed), 13)
    return {
        "tokens": scatter_about(key_list[0], (ROWS, SEQ, D), 1.0, 6.0, ((0, 2), (1, 16))),
        "lengths": jax.vmap(lambda own: uneven_parts(own, NDOC, SEQ, SEQ - TOK_CTX // 2, 2))(jax.random.split(key_list[1], ROWS)).reshape((ROWS, NDOC)).astype(jnp.int32),
        "q_weight": scatter_about(key_list[2], (D, HEADS * HEAD), (D // 2) ** -0.5, 0.1875, ((1, 4),)),
        "k_weight": scatter_about(key_list[3], (D, KV_HEADS * HEAD), (D // 2) ** -0.5, 0.1875, ((1, 4),)),
        "v_weight": scatter_about(key_list[4], (D, KV_HEADS * HEAD), D ** -0.5, 0.125, ((1, 4),)),
        "o_weight": scatter_about(key_list[5], (HEADS * HEAD, D), (HEADS * HEAD // 64) ** -0.5, 1.0, ((0, 4),)),
        "gate_weight": scatter_about(key_list[6], (D, FF), D ** -0.5, 0.125, ((1, 4),)),
        "up_weight": scatter_about(key_list[7], (D, FF), D ** -0.5, 0.125, ((1, 4),)),
        "down_weight": scatter_about(key_list[8], (FF, D), FF ** -0.5, 0.0625, ((0, 4),)),
        "attention_norm_gain": jnp.clip(1.0 + 0.1 * jax.random.normal(key_list[9], (D,), jnp.float32), 0.5, 1.5),
        "feedforward_norm_gain": jnp.clip(1.0 + 0.1 * jax.random.normal(key_list[10], (D,), jnp.float32), 0.5, 1.5),
        "cotangent": scatter_about(key_list[11], (ROWS, SEQ, D), 1.0, 6.0, ((0, 2), (1, 16))),
    }


@jax.custom_vjp
def low(v):
    return lax.optimization_barrier(v.astype(jnp.bfloat16)).astype(jnp.float32)

@jax.custom_vjp
def low_back(v):
    return v

def low_keep(v):
    return (low(v), None)

def low_pass(kept, grad):
    return (grad,)

def back_keep(v):
    return (v, None)

def back_low(kept, grad):
    return (low(grad),)
low.defvjp(low_keep, low_pass)
low_back.defvjp(back_keep, back_low)
epsilon = 1e-05
negative = -1e+30
highest = lax.Precision.HIGHEST

def rope_angles(positions, head_size):
    half = head_size // 2
    steps = jnp.arange(half, dtype=jnp.float32)
    base = jnp.power(jnp.float32(500000.0), -2.0 * steps / head_size)
    wavelen = 2.0 * math.pi / base
    smooth = (8192.0 / wavelen - 1.0) / 3.0
    residual_between = (1.0 - smooth) * base / 32.0 + smooth * base
    gain_scaled_rows = jnp.where(wavelen > 8192.0, base / 32.0, jnp.where(wavelen < 2048.0, base, residual_between))
    angle = positions.astype(jnp.float32)[:, None] * gain_scaled_rows[None, :]
    return (jnp.cos(angle), jnp.sin(angle))

def rotate(values, cosine, sine):
    half = values.shape[-1] // 2
    first = values[..., :half]
    second = values[..., half:]
    cos_b = cosine[:, None, :]
    sin_b = sine[:, None, :]
    return jnp.concatenate([first * cos_b - second * sin_b, second * cos_b + first * sin_b], -1)

def doc_layout(lengths_row, index):
    lengths_row = lengths_row.astype(jnp.int32)
    ends = jnp.cumsum(lengths_row).astype(jnp.int32)
    starts = ends - lengths_row
    segment = lax.optimization_barrier(jnp.sum((index[:, None] >= ends[None, :]).astype(jnp.int32), 1)).astype(jnp.int32)
    docs = jnp.arange(lengths_row.shape[0], dtype=jnp.int32)
    first = lax.optimization_barrier(jnp.sum(jnp.where(segment[:, None] == docs[None, :], starts[None, :], 0), 1)).astype(jnp.int32)
    return (segment, index - first)

def linear(left, weight):
    return jnp.dot(left, weight, precision=highest, preferred_element_type=jnp.float32)

def attend_rows(queries, keys, values, q_segment, q_index, k_segment, k_index):
    scores = jnp.einsum('qkgd,nkd->kgqn', queries, keys, precision=highest) * HEAD ** (-0.5)
    scores = low_back(scores)
    allowed = (q_segment[:, None] == k_segment[None, :]) & (q_index[:, None] >= k_index[None, :])
    scores = jnp.where(allowed[None, None], scores, negative)
    peak = lax.optimization_barrier(jnp.max(scores, -1, keepdims=True))
    weights = jnp.exp(scores - peak)
    probs = low(weights / lax.optimization_barrier(jnp.sum(weights, -1, keepdims=True)))
    result = jnp.einsum('kgqn,nkd->qkgd', probs, values, precision=highest)
    return result.reshape(result.shape[0], -1)

def layer_row(x_row, segment, position, q_weight, k_weight, v_weight, o_weight, gate_weight, up_weight, down_weight, attention_norm_gain, feedforward_norm_gain):
    length = x_row.shape[0]
    share = HEADS // KV_HEADS
    index = jnp.arange(length, dtype=jnp.int32)
    cosine, sine = rope_angles(position, HEAD)
    inverse_root_first = lax.rsqrt(lax.optimization_barrier(jnp.mean(x_row * x_row, -1, keepdims=True)) + epsilon)
    attention_normalized = low(x_row * inverse_root_first * attention_norm_gain)
    queries = low_back(linear(attention_normalized, q_weight)).reshape(length, HEADS, HEAD)
    queries = low(rotate(queries, cosine, sine)).reshape(length, KV_HEADS, share, HEAD)
    keys = low_back(linear(attention_normalized, k_weight)).reshape(length, KV_HEADS, HEAD)
    keys = low(rotate(keys, cosine, sine))
    values = low(low_back(linear(attention_normalized, v_weight))).reshape(length, KV_HEADS, HEAD)
    block = min(length, 512)
    count = length // block

    def one_block(pieces):
        q_block, s_block, i_block = pieces
        return attend_rows(q_block, keys, values, s_block, i_block, segment, index)
    attended = lax.map(jax.checkpoint(one_block), (queries.reshape(count, block, KV_HEADS, share, HEAD), segment.reshape(count, block), index.reshape(count, block)))
    attended = low(low_back(attended.reshape(length, HEADS * HEAD)))
    residual_between = x_row + low_back(linear(attended, o_weight))
    inverse_root_second = lax.rsqrt(lax.optimization_barrier(jnp.mean(residual_between * residual_between, -1, keepdims=True)) + epsilon)
    feedforward_normalized = low(residual_between * inverse_root_second * feedforward_norm_gain)
    gate_value = low_back(linear(feedforward_normalized, gate_weight))
    up_value = low_back(linear(feedforward_normalized, up_weight))
    activ = low(gate_value * jax.nn.sigmoid(gate_value) * up_value)
    return residual_between + low_back(linear(activ, down_weight))

def reference(tokens, lengths, q_weight, k_weight, v_weight, o_weight, gate_weight, up_weight, down_weight, attention_norm_gain, feedforward_norm_gain, cotangent):
    index = jnp.arange(SEQ, dtype=jnp.int32)
    segment, position = jax.vmap(lambda row: doc_layout(row, index))(lengths)
    weights = tuple((w.astype(jnp.float32) for w in (q_weight, k_weight, v_weight, o_weight, gate_weight, up_weight, down_weight, attention_norm_gain, feedforward_norm_gain)))

    def forward(inputs, *params):

        def one_row(pieces):
            x_row, seg_row, pos_row = pieces
            return layer_row(x_row, seg_row, pos_row, *params)
        return lax.map(one_row, (inputs, segment, position))
    result, pull = jax.vjp(forward, tokens.astype(jnp.float32), *weights)
    grads = pull(cotangent.astype(jnp.float32))
    return (result.astype(jnp.bfloat16), grads[0].astype(jnp.bfloat16), grads[1], grads[2], grads[3], grads[4], grads[5], grads[6], grads[7], grads[8], grads[9])
```

```python
import functools
import math

import jax
import jax.numpy as jnp
from jax import lax
from jax.experimental import pallas as pl
from jax.experimental.pallas import tpu as pltpu
from jax.sharding import PartitionSpec as P

HEAD = 64
LANES = 128
epsilon = 1e-05
negative = -1e30
plain = (((1,), (0,)), ((), ()))
contract_first = (((0,), (0,)), ((), ()))
contract_last = (((1,), (1,)), ((), ()))
bf16 = jnp.bfloat16
f32 = jnp.float32
barrier = lax.optimization_barrier


def dot(left, right, dims=plain):
    return lax.dot_general(left, right, dims, preferred_element_type=f32)


def rope_tables(positions):
    half = HEAD // 2
    steps = jnp.arange(half, dtype=f32)
    base = jnp.power(f32(500000.0), -2.0 * steps / HEAD)
    wavelen = 2.0 * math.pi / base
    smooth = (8192.0 / wavelen - 1.0) / 3.0
    between = (1.0 - smooth) * base / 32.0 + smooth * base
    used = jnp.where(wavelen > 8192.0, base / 32.0, jnp.where(wavelen < 2048.0, base, between))
    angle = positions.astype(f32)[:, None] * jnp.tile(used, LANES // half)[None, :]
    sign = jnp.where(jnp.arange(LANES) % HEAD < half, -1.0, 1.0).astype(f32)
    return jnp.cos(angle), jnp.sin(angle) * sign[None, :]


def doc_starts(lengths_row, index):
    count = lengths_row.shape[0]
    docs = jnp.arange(count, dtype=jnp.int32)
    ends = jnp.sum(jnp.where(docs[None, :] <= docs[:, None], lengths_row[None, :], 0), 1)
    return jnp.max(jnp.where(index[:, None] >= ends[None, :], ends[None, :], 0), 1)


def swap_halves(v):
    lane = lax.broadcasted_iota(jnp.int32, v.shape, 1)
    return jnp.where(lane % HEAD < HEAD // 2, pltpu.roll(v, LANES - HEAD // 2, 1), pltpu.roll(v, HEAD // 2, 1))


def rope_kernel(q_cols, turned, x_ref, cos_ref, sin_ref, out_ref):
    cosine, sine = cos_ref[...], sin_ref[...]
    lane = lax.broadcasted_iota(jnp.int32, cosine.shape, 1)
    for at in range(0, x_ref.shape[1], LANES):
        v = x_ref[:, at : at + LANES].astype(f32)
        if at < turned:
            r = v * cosine + swap_halves(v) * sine
            v = r if at + LANES <= turned else jnp.where(lane < turned - at, r, v)
            if at < q_cols:
                v = v * HEAD**-0.5
        out_ref[:, at : at + LANES] = v.astype(bf16)


def rope(x, cosine, sine, q_cols, turned):
    rows, cols = x.shape
    step = min(rows, 256)
    return pl.pallas_call(
        functools.partial(rope_kernel, q_cols, turned),
        grid=(rows // step,),
        in_specs=[
            pl.BlockSpec((step, cols), lambda i: (i, 0)),
            pl.BlockSpec((step, LANES), lambda i: (i, 0)),
            pl.BlockSpec((step, LANES), lambda i: (i, 0)),
        ],
        out_specs=pl.BlockSpec((step, cols), lambda i: (i, 0)),
        out_shape=jax.ShapeDtypeStruct((rows, cols), bf16),
        name="rotate",
    )(x, cosine, sine)


def spread_head(kv_ref, offset, out):
    at = offset // LANES * LANES
    here = kv_ref[:, at : at + LANES].astype(f32)
    there = pltpu.roll(here, HEAD, 1)
    if offset % LANES:
        here, there = there, here
    left = lax.broadcasted_iota(jnp.int32, here.shape, 1) < HEAD
    out[0] = jnp.where(left, here, 0.0).astype(bf16)
    out[1] = jnp.where(left, 0.0, there).astype(bf16)


def spread_heads(kv, per, kv_ref, k_pad, v_pad):
    for g in range(kv):

        @pl.when((pl.program_id(0) == g * per) & (pl.program_id(1) == 0))
        def _():
            spread_head(kv_ref, g * HEAD, k_pad)
            spread_head(kv_ref, (kv + g) * HEAD, v_pad)


def over_blocks(bounds, block, step, carry):
    b0, b1, b2, b3 = [bounds[1 + k, block] for k in range(4)]
    carry = lax.fori_loop(b0, b1, functools.partial(step, True), carry)
    carry = lax.fori_loop(b1, b2, functools.partial(step, False), carry)
    return lax.fori_loop(b2, b3, functools.partial(step, True), carry)


def allowed_keys(at, first_row, low, bk, bq):
    key = at + lax.broadcasted_iota(jnp.int32, (bk, bq), 0)
    row = first_row + lax.broadcasted_iota(jnp.int32, (bk, bq), 1)
    return (key <= row) & (key >= low)


def attend_kernel(bq, bk, kv, per, bounds, q_ref, kv_ref, low_ref, o_ref, lse_ref, k_pad, v_pad):
    block = pl.program_id(1)
    spread_heads(kv, per, kv_ref, k_pad, v_pad)
    q = q_ref[...]
    upper = lax.broadcasted_iota(jnp.int32, (LANES, bq), 0) < HEAD

    def step(masked, j, carry):
        peaks, totals, acc = carry
        at = pl.multiple_of(j * bk, bk)
        if masked:
            ok = allowed_keys(at, bounds[0, block], low_ref[:1, :], bk, bq)
        new_peaks, new_totals, decays, parts = [], [], [], []
        for h in range(2):
            s = dot(k_pad[h, pl.ds(at, bk), :], q, contract_last)
            if masked:
                s = jnp.where(ok, s, negative)
            peak = jnp.maximum(peaks[h], jnp.max(s, 0, keepdims=True))
            p = jnp.exp(s - peak)
            if masked:
                p = jnp.where(ok, p, 0.0)
            decay = jnp.exp(peaks[h] - peak)
            new_peaks.append(peak)
            new_totals.append(totals[h] * decay + jnp.sum(p, 0, keepdims=True))
            decays.append(decay)
            parts.append(dot(v_pad[h, pl.ds(at, bk), :], p.astype(bf16), contract_first))
        acc = acc * jnp.where(upper, *decays) + parts[0] + parts[1]
        return tuple(new_peaks), tuple(new_totals), acc

    low_row = jnp.full((1, bq), negative, f32)
    zero_row = jnp.zeros((1, bq), f32)
    start = ((low_row, low_row), (zero_row, zero_row), jnp.zeros((LANES, bq), f32))
    peaks, totals, acc = over_blocks(bounds, block, step, start)
    o_ref[...] = (acc / jnp.where(upper, *totals)).T.astype(bf16)
    for h in range(2):
        lse_ref[0, h : h + 1, :] = peaks[h] + jnp.log(totals[h])


def attend_back_kernel(
    bq, bk, kv, per, blocks, bounds, q_ref, do_ref, o_ref, kv_ref, low_ref, lse_ref, cos_ref, sin_ref,
    dq_ref, dkv_ref, k_pad, v_pad, dk_acc, dv_acc,
):
    pair, block = pl.program_id(0), pl.program_id(1)
    spread_heads(kv, per, kv_ref, k_pad, v_pad)

    @pl.when((pair % per == 0) & (block == 0))
    def _():
        dk_acc[...] = jnp.zeros_like(dk_acc)
        dv_acc[...] = jnp.zeros_like(dv_acc)

    q, do = q_ref[...], do_ref[...]
    left = lax.broadcasted_iota(jnp.int32, (bq, LANES), 1) < HEAD
    zero = jnp.zeros_like(q)
    q_of = (jnp.where(left, q, zero), jnp.where(left, zero, q))
    do_of = (jnp.where(left, do, zero), jnp.where(left, zero, do))
    product = do.astype(f32) * o_ref[...].astype(f32)
    high = product.astype(bf16)
    rest = (product - high.astype(f32)).astype(bf16)
    row = lax.broadcasted_iota(jnp.int32, (8, LANES), 0)
    lane = lax.broadcasted_iota(jnp.int32, (8, LANES), 1)
    ones = jnp.where(lane // HEAD == row, 1.0, 0.0).astype(bf16)
    delta = dot(ones, high, contract_last) + dot(ones, rest, contract_last)

    def step(masked, j, acc):
        at = pl.multiple_of(j * bk, bk)
        if masked:
            ok = allowed_keys(at, bounds[0, block], low_ref[:1, :], bk, bq)
        dk, dv = [], []
        for h in range(2):
            k, v = k_pad[h, pl.ds(at, bk), :], v_pad[h, pl.ds(at, bk), :]
            p = jnp.exp(dot(k, q, contract_last) - lse_ref[0, h : h + 1, :])
            if masked:
                p = jnp.where(ok, p, 0.0)
            ds = (p * (dot(v, do, contract_last) - delta[h : h + 1, :])).astype(bf16)
            dv.append(dot(p.astype(bf16), do_of[h]))
            dk.append(dot(ds, q_of[h]))
            acc = acc + dot(ds, k, contract_first)
        dk_acc[pl.ds(at, bk), :] += dk[0] + dk[1]
        dv_acc[pl.ds(at, bk), :] += dv[0] + dv[1]
        return acc

    g = over_blocks(bounds, block, step, jnp.zeros((bq, LANES), f32))
    dq_ref[...] = ((g * cos_ref[...] - swap_halves(g) * sin_ref[...]) * HEAD**-0.5).astype(bf16)

    for g in range(kv):

        @pl.when((pair == (g + 1) * per - 1) & (block == blocks - 1))
        def _():
            for acc, offset in ((dk_acc, g * HEAD), (dv_acc, (kv + g) * HEAD)):
                both = acc[...]
                both = (both + pltpu.roll(both, HEAD, 1)).astype(bf16)
                at = offset // LANES * LANES
                if offset % LANES:
                    keep = lax.broadcasted_iota(jnp.int32, both.shape, 1) < HEAD
                    both = jnp.where(keep, dkv_ref[:, at : at + LANES], both)
                dkv_ref[:, at : at + LANES] = both


def attention_calls(rows, cols, keys, kv, bq, bk):
    pairs, blocks = cols // LANES, rows // bq
    per = pairs // kv
    heads = pl.BlockSpec((bq, LANES), lambda p, i, b: (i, p))
    table = pl.BlockSpec((bq, LANES), lambda p, i, b: (i, 0))
    whole = pl.BlockSpec((keys, 2 * kv * HEAD), lambda p, i, b: (0, 0))
    low = pl.BlockSpec((8, bq), lambda p, i, b: (0, i))
    sums = pl.BlockSpec((1, 8, bq), lambda p, i, b: (p, 0, i))
    pads = [pltpu.VMEM((2, keys, LANES), bf16)] * 2
    params = pltpu.CompilerParams(vmem_limit_bytes=60 * 2**20)
    size = rows * cols * keys
    forward = pl.pallas_call(
        functools.partial(attend_kernel, bq, bk, kv, per),
        grid_spec=pltpu.PrefetchScalarGridSpec(
            num_scalar_prefetch=1, grid=(pairs, blocks), in_specs=[heads, whole, low],
            out_specs=[heads, sums], scratch_shapes=pads,
        ),
        out_shape=[
            jax.ShapeDtypeStruct((rows, cols), bf16),
            jax.ShapeDtypeStruct((pairs, 8, rows), f32),
        ],
        compiler_params=params,
        cost_estimate=pl.CostEstimate(flops=8 * size, bytes_accessed=8 * rows * cols, transcendentals=size // HEAD),
        name="attend",
    )
    backward = pl.pallas_call(
        functools.partial(attend_back_kernel, bq, bk, kv, per, blocks),
        grid_spec=pltpu.PrefetchScalarGridSpec(
            num_scalar_prefetch=1, grid=(pairs, blocks),
            in_specs=[heads, heads, heads, whole, low, sums, table, table],
            out_specs=[heads, whole],
            scratch_shapes=pads + [pltpu.VMEM((keys, LANES), f32)] * 2,
        ),
        out_shape=[
            jax.ShapeDtypeStruct((rows, cols), bf16),
            jax.ShapeDtypeStruct((keys, 2 * kv * HEAD), bf16),
        ],
        compiler_params=params,
        cost_estimate=pl.CostEstimate(flops=16 * size, bytes_accessed=8 * rows * cols, transcendentals=size // HEAD),
        name="attend_back",
    )
    return forward, backward


def block_bounds(starts, low, bq, bk):
    low = low.reshape(-1, bq)
    begin, end = low[:, 0] // bk, (starts + bq + bk - 1) // bk
    whole = jnp.clip((low[:, -1] + bk - 1) // bk, begin, end)
    diagonal = jnp.clip((starts + 1) // bk, whole, end)
    return jnp.stack([starts, begin, whole, diagonal, end]).astype(jnp.int32)


def bits_of(n):
    return [1 << b for b in range(n.bit_length() - 1)]


def exchange(x, axis, bit):
    n = lax.axis_size(axis)
    return lax.ppermute(x, axis, [(i, i ^ bit) for i in range(n)])


def gather_ctx(x):
    n, me = lax.axis_size("ctx"), lax.axis_index("ctx")
    held = {0: x}
    for bit in reversed(bits_of(n)):
        held.update({mask ^ bit: exchange(piece, "ctx", bit) for mask, piece in held.items()})
    out = jnp.zeros((n, *x.shape), x.dtype)
    for mask, piece in held.items():
        out = lax.dynamic_update_index_in_dim(out, piece, me ^ mask, 0)
    return out.reshape(-1, x.shape[1])


def scatter_sum_ctx(x):
    n, me = lax.axis_size("ctx"), lax.axis_index("ctx")
    x = x.reshape(n, -1, x.shape[1])
    for bit in bits_of(n):
        x = x.reshape(-1, 2, *x.shape[1:])
        mine = (me // bit) % 2
        send = lax.dynamic_index_in_dim(x, 1 - mine, 1, False)
        keep = lax.dynamic_index_in_dim(x, mine, 1, False)
        x = (keep.astype(f32) + exchange(send, "ctx", bit).astype(f32)).astype(bf16)
    return x[0]


def mirror_ctx(x):
    n = lax.axis_size("ctx")
    return lax.ppermute(x, "ctx", [(i, n - 1 - i) for i in range(n)])


def norm_back(grad, unit, inverse_root, gain):
    scaled = grad * gain
    return inverse_root * (scaled - unit * jnp.mean(scaled * unit, -1, keepdims=True))


def gather_tp(x):
    return lax.all_gather(x, "tp", axis=0, tiled=True)


def scatter_tp(x):
    return lax.psum_scatter(x, "tp", scatter_dimension=0, tiled=True)


def on_device(
    tokens, lengths, q_weight, k_weight, v_weight, o_weight, gate_weight, up_weight, down_weight,
    attention_gain, ffn_gain, cotangent,
):
    ctx, me = lax.axis_size("ctx"), lax.axis_index("ctx")
    own = tokens.shape[1]
    block = own * lax.axis_size("tp")
    half = block // 2
    keys = block * ctx
    q_cols, kv_cols = q_weight.shape[1], k_weight.shape[1]
    kv = kv_cols // HEAD

    x = tokens[0].astype(f32)
    rstd1 = lax.rsqrt(jnp.mean(x * x, -1, keepdims=True) + epsilon)
    unit1 = x * rstd1
    normed = gather_tp((unit1 * attention_gain).astype(bf16))

    index = me * block + jnp.arange(block, dtype=jnp.int32)
    cosine, sine = rope_tables(index - doc_starts(lengths[0], index))
    far = (2 * ctx - 1 - 2 * me) * half
    near = me * block
    steps = jnp.arange(half, dtype=jnp.int32)
    q_index = jnp.concatenate([near + steps, far + steps])
    q_low = doc_starts(lengths[0], q_index)
    q_cos, q_sin = rope_tables(q_index - q_low)
    bq = bk = min(512, half)
    bounds = block_bounds(q_index.reshape(-1, bq)[:, 0], q_low, bq, bk)
    low_rows = jnp.broadcast_to(q_low[None, :], (8, block))
    attend, attend_back = attention_calls(block, q_cols, keys, kv, bq, bk)

    w_qkv = jnp.concatenate([q_weight, k_weight, v_weight], 1)
    turned = rope(dot(normed, w_qkv), cosine, sine, q_cols, q_cols + kv_cols)
    kv_all = gather_ctx(turned[:, q_cols:])
    queries = jnp.concatenate([turned[:half, :q_cols], mirror_ctx(turned[half:, :q_cols])], 0)
    attended_z, log_sums = attend(bounds, queries, kv_all, low_rows)
    attended = jnp.concatenate([attended_z[:half], mirror_ctx(attended_z[half:])], 0)

    mid = x + scatter_tp(dot(attended, o_weight).astype(bf16)).astype(f32)
    rstd2 = lax.rsqrt(jnp.mean(mid * mid, -1, keepdims=True) + epsilon)
    unit2 = mid * rstd2
    ffn_normed = gather_tp((unit2 * ffn_gain).astype(bf16))
    c_own, _ = barrier((cotangent[0], normed))
    c_full = gather_tp(c_own)

    gate = dot(ffn_normed, gate_weight)
    up = dot(ffn_normed, up_weight)
    sig = jax.nn.sigmoid(gate)
    swish = gate * sig
    act = (swish * up).astype(bf16)
    d_act = dot(c_full, down_weight, contract_last)
    d_gate = (d_act * up * sig * (1.0 + gate * (1.0 - sig))).astype(bf16)
    d_up = (d_act * swish).astype(bf16)
    d_ffn_part = (dot(d_gate, gate_weight, contract_last) + dot(d_up, up_weight, contract_last)).astype(bf16)
    d_ffn = scatter_tp(d_ffn_part).astype(f32)
    d_mid = c_own.astype(f32) + norm_back(d_ffn, unit2, rstd2, ffn_gain)
    ffn_gain_part = jnp.sum(d_ffn * unit2, 0)
    d_branch = gather_tp(d_mid.astype(bf16))

    act_late, _ = barrier((act, d_branch))
    output = (mid + scatter_tp(dot(act_late, down_weight).astype(bf16)).astype(f32)).astype(bf16)[None]

    d_down = dot(act, c_full, contract_first)
    d_gate_w = dot(ffn_normed, d_gate, contract_first)
    d_up_w = dot(ffn_normed, d_up, contract_first)

    d_o = dot(attended, d_branch, contract_first)
    d_attended = dot(d_branch, o_weight, contract_last).astype(bf16)
    d_attended = jnp.concatenate([d_attended[:half], mirror_ctx(d_attended[half:])], 0)
    d_q, d_kv = attend_back(
        bounds, queries, d_attended, attended_z, kv_all, low_rows, log_sums, q_cos, q_sin
    )
    d_q = jnp.concatenate([d_q[:half], mirror_ctx(d_q[half:])], 0)
    d_kv = rope(scatter_sum_ctx(d_kv), cosine, -sine, 0, kv_cols)
    d_qkv = jnp.concatenate([d_q, d_kv], 1)
    d_qkv_w = dot(normed, d_qkv, contract_first)
    d_normed = scatter_tp(dot(d_qkv, w_qkv, contract_last).astype(bf16)).astype(f32)
    input_gradient = (d_mid + norm_back(d_normed, unit1, rstd1, attention_gain)).astype(bf16)[None]
    attn_gain_part = jnp.sum(d_normed * unit1, 0)

    d_gains = lax.psum((attn_gain_part, ffn_gain_part), ("dp", "ctx", "tp"))
    grads = [
        lax.psum(g.astype(bf16), ("dp", "ctx")).astype(f32)
        for g in (
            d_qkv_w[:, :q_cols], d_qkv_w[:, q_cols : q_cols + kv_cols], d_qkv_w[:, q_cols + kv_cols :],
            d_o, d_gate_w, d_up_w, d_down,
        )
    ]
    return (output, input_gradient, *grads, *d_gains)


def solution(mesh):
    rows = P("dp", ("ctx", "tp"), None)
    columns, across = P(None, "tp"), P("tp", None)
    return jax.shard_map(
        on_device,
        mesh=mesh,
        in_specs=(
            rows, P("dp", None), columns, columns, columns, across, columns, columns, across, P(), P(), rows,
        ),
        out_specs=(rows, rows, columns, columns, columns, across, columns, columns, across, P(), P()),
        check_vma=False,
    )
```

```python
import functools
import math

import jax
import jax.numpy as jnp
from jax import lax
from jax.experimental import pallas as pl
from jax.experimental.pallas import tpu as pltpu
from jax.sharding import PartitionSpec as P

HEAD = 64
LANES = 128
epsilon = 1e-05
negative = -1e30
plain = (((1,), (0,)), ((), ()))
contract_first = (((0,), (0,)), ((), ()))
contract_last = (((1,), (1,)), ((), ()))
bf16 = jnp.bfloat16
f32 = jnp.float32
barrier = lax.optimization_barrier
CHUNKS = 2


def dot(left, right, dims=plain):
    return lax.dot_general(left, right, dims, preferred_element_type=f32)


def rope_tables(positions):
    half = HEAD // 2
    steps = jnp.arange(half, dtype=f32)
    base = jnp.power(f32(500000.0), -2.0 * steps / HEAD)
    wavelen = 2.0 * math.pi / base
    smooth = (8192.0 / wavelen - 1.0) / 3.0
    between = (1.0 - smooth) * base / 32.0 + smooth * base
    used = jnp.where(wavelen > 8192.0, base / 32.0, jnp.where(wavelen < 2048.0, base, between))
    angle = positions.astype(f32)[:, None] * jnp.tile(used, LANES // half)[None, :]
    sign = jnp.where(jnp.arange(LANES) % HEAD < half, -1.0, 1.0).astype(f32)
    return jnp.cos(angle), jnp.sin(angle) * sign[None, :]


def doc_starts(lengths_row, index):
    count = lengths_row.shape[0]
    docs = jnp.arange(count, dtype=jnp.int32)
    ends = jnp.sum(jnp.where(docs[None, :] <= docs[:, None], lengths_row[None, :], 0), 1)
    return jnp.max(jnp.where(index[:, None] >= ends[None, :], ends[None, :], 0), 1)


def swap_halves(v):
    lane = lax.broadcasted_iota(jnp.int32, v.shape, 1)
    return jnp.where(lane % HEAD < HEAD // 2, pltpu.roll(v, LANES - HEAD // 2, 1), pltpu.roll(v, HEAD // 2, 1))


def rope_kernel(q_cols, turned, x_ref, cos_ref, sin_ref, out_ref):
    cosine, sine = cos_ref[...], sin_ref[...]
    lane = lax.broadcasted_iota(jnp.int32, cosine.shape, 1)
    for at in range(0, x_ref.shape[1], LANES):
        v = x_ref[:, at : at + LANES].astype(f32)
        if at < turned:
            r = v * cosine + swap_halves(v) * sine
            v = r if at + LANES <= turned else jnp.where(lane < turned - at, r, v)
            if at < q_cols:
                v = v * HEAD**-0.5
        out_ref[:, at : at + LANES] = v.astype(bf16)


def rope(x, cosine, sine, q_cols, turned):
    rows, cols = x.shape
    step = min(rows, 256)
    return pl.pallas_call(
        functools.partial(rope_kernel, q_cols, turned),
        grid=(rows // step,),
        in_specs=[
            pl.BlockSpec((step, cols), lambda i: (i, 0)),
            pl.BlockSpec((step, LANES), lambda i: (i, 0)),
            pl.BlockSpec((step, LANES), lambda i: (i, 0)),
        ],
        out_specs=pl.BlockSpec((step, cols), lambda i: (i, 0)),
        out_shape=jax.ShapeDtypeStruct((rows, cols), bf16),
        name="rotate",
    )(x, cosine, sine)


def project_kernel(q_cols, turned, x_ref, w_ref, cos_ref, sin_ref, out_ref, sums):
    sums[...] = dot(x_ref[...], w_ref[...])
    rope_kernel(q_cols, turned, sums, cos_ref, sin_ref, out_ref)


def project(x, w, cosine, sine, q_cols, turned):
    rows, depth = x.shape
    cols = w.shape[1]
    step = min(rows, 256)
    return pl.pallas_call(
        functools.partial(project_kernel, q_cols, turned),
        grid=(rows // step,),
        in_specs=[
            pl.BlockSpec((step, depth), lambda i: (i, 0)),
            pl.BlockSpec((depth, cols), lambda i: (0, 0)),
            pl.BlockSpec((step, LANES), lambda i: (i, 0)),
            pl.BlockSpec((step, LANES), lambda i: (i, 0)),
        ],
        out_specs=pl.BlockSpec((step, cols), lambda i: (i, 0)),
        out_shape=jax.ShapeDtypeStruct((rows, cols), bf16),
        scratch_shapes=[pltpu.VMEM((step, cols), f32)],
        compiler_params=pltpu.CompilerParams(vmem_limit_bytes=40 * 2**20),
        cost_estimate=pl.CostEstimate(flops=2 * rows * depth * cols, bytes_accessed=2 * rows * depth, transcendentals=0),
        name="project",
    )(x, w, cosine, sine)


def spread_kernel(kv, n, here, *refs):
    pieces, (both_ref, turned_ref) = refs[:n], refs[n:]
    for mask, piece in enumerate(pieces):
        rows = piece.shape[0]
        place = pl.ds(pl.multiple_of((here[0] ^ mask) * rows, rows), rows)
        for at in range(0, piece.shape[1], LANES):
            x = piece[:, at : at + LANES].astype(f32)
            other = pltpu.roll(x, HEAD, 1)
            left = lax.broadcasted_iota(jnp.int32, x.shape, 1) < HEAD
            head = at // HEAD
            both_ref[head, place, :] = jnp.where(left, x, other).astype(bf16)
            both_ref[head + 1, place, :] = jnp.where(left, other, x).astype(bf16)
            turned_ref[at : at + LANES, place] = x.T.astype(bf16)


def spread(here, pieces, kv):
    n, (rows, cols) = len(pieces), pieces[0].shape
    return pl.pallas_call(
        functools.partial(spread_kernel, kv, n),
        grid_spec=pltpu.PrefetchScalarGridSpec(
            num_scalar_prefetch=1, grid=(1,),
            in_specs=[pl.BlockSpec((rows, cols), lambda i, h: (0, 0))] * n,
            out_specs=[
                pl.BlockSpec((2 * kv, n * rows, LANES), lambda i, h: (0, 0, 0)),
                pl.BlockSpec((cols, n * rows), lambda i, h: (0, 0)),
            ],
        ),
        out_shape=[
            jax.ShapeDtypeStruct((2 * kv, n * rows, LANES), bf16),
            jax.ShapeDtypeStruct((cols, n * rows), bf16),
        ],
        compiler_params=pltpu.CompilerParams(vmem_limit_bytes=60 * 2**20),
        name="spread",
    )(here, *pieces)


def over_blocks(bounds, block, step, carry):
    b0, b1, b2, b3 = [bounds[1 + k, block] for k in range(4)]
    carry = lax.fori_loop(b0, b1, functools.partial(step, True), carry)
    carry = lax.fori_loop(b1, b2, functools.partial(step, False), carry)
    return lax.fori_loop(b2, b3, functools.partial(step, True), carry)


def allowed_keys(at, first_row, low, bk, bq):
    key = at + lax.broadcasted_iota(jnp.int32, (bk, bq), 0)
    row = first_row + lax.broadcasted_iota(jnp.int32, (bk, bq), 1)
    return (key <= row) & (key >= low)


def halves(x):
    left = lax.broadcasted_iota(jnp.int32, x.shape, 1) < HEAD
    zero = jnp.zeros_like(x)
    return [jnp.where(left, x, zero), jnp.where(left, zero, x)]


def attend_kernel(bq, bk, bounds, q_ref, low_ref, k_ref, vt_ref, o_ref, lse_ref):
    block = pl.program_id(0)
    pairs = q_ref.shape[1] // LANES
    heads = range(2 * pairs)
    q = sum([halves(q_ref[:, p * LANES : (p + 1) * LANES]) for p in range(pairs)], [])

    def step(masked, j, carry):
        peaks, totals, accs = carry
        at = pl.multiple_of(j * bk, bk)
        if masked:
            ok = allowed_keys(at, bounds[0, block], low_ref[:1, :], bk, bq)
        k = k_ref[0, pl.ds(at, bk), :]
        scores = [dot(k, q[h], contract_last) for h in heads]
        new_peaks, new_totals, new_accs = [], [], []
        for h in heads:
            s = scores[h]
            if masked:
                s = jnp.where(ok, s, negative)
            peak = jnp.maximum(peaks[h], jnp.max(s, 0, keepdims=True))
            p = jnp.exp(s - peak)
            if masked:
                p = jnp.where(ok, p, 0.0)
            decay = jnp.exp(peaks[h] - peak)
            new_peaks.append(peak)
            new_totals.append(totals[h] * decay + jnp.sum(p, 0, keepdims=True))
            new_accs.append(accs[h] * decay + dot(vt_ref[:, pl.ds(at, bk)], p.astype(bf16)))
        return tuple(new_peaks), tuple(new_totals), tuple(new_accs)

    start = [(jnp.full((1, bq), negative, f32),) * len(heads), (jnp.zeros((1, bq), f32),) * len(heads)]
    start.append((jnp.zeros((HEAD, bq), f32),) * len(heads))
    peaks, totals, accs = over_blocks(bounds, block, step, tuple(start))
    for p in range(pairs):
        pair = [accs[h] / totals[h] for h in (2 * p, 2 * p + 1)]
        o_ref[:, p * LANES : (p + 1) * LANES] = jnp.concatenate(pair, 0).T.astype(bf16)
    for h in heads:
        lse_ref[h // 2, h % 2 : h % 2 + 1, :] = peaks[h] + jnp.log(totals[h])


def attend(bounds, queries, low, both, turned, g, kv, bq, bk):
    rows, keys = queries.shape[0], both.shape[1]
    cols = queries.shape[1] // kv
    pairs = cols // LANES
    size = rows * cols * keys
    return pl.pallas_call(
        functools.partial(attend_kernel, bq, bk),
        grid_spec=pltpu.PrefetchScalarGridSpec(
            num_scalar_prefetch=1, grid=(rows // bq,),
            in_specs=[
                pl.BlockSpec((bq, cols), lambda i, b: (i, g)),
                pl.BlockSpec((8, bq), lambda i, b: (0, i)),
                pl.BlockSpec((1, keys, LANES), lambda i, b: (g, 0, 0)),
                pl.BlockSpec((HEAD, keys), lambda i, b: (kv + g, 0)),
            ],
            out_specs=[
                pl.BlockSpec((bq, cols), lambda i, b: (i, 0)),
                pl.BlockSpec((pairs, 8, bq), lambda i, b: (0, 0, i)),
            ],
        ),
        out_shape=[
            jax.ShapeDtypeStruct((rows, cols), bf16),
            jax.ShapeDtypeStruct((pairs, 8, rows), f32),
        ],
        compiler_params=pltpu.CompilerParams(vmem_limit_bytes=60 * 2**20),
        cost_estimate=pl.CostEstimate(flops=28 * size, bytes_accessed=8 * rows * cols, transcendentals=size // HEAD),
        name="attend",
    )(bounds, queries, low, both, turned)


def attend_back_kernel(
    bq, bk, pieces, bounds, q_ref, o_ref, low_ref, lse_ref, cos_ref, sin_ref, k_ref, kt_ref, v_ref, *rest
):
    do_refs, (dq_ref, dk_ref, dv_ref, do_rows) = rest[:pieces], rest[pieces:]
    pair, block = pl.program_id(0), pl.program_id(1)

    @pl.when((pair == 0) & (block == 0))
    def _():
        dk_ref[...] = jnp.zeros_like(dk_ref)
        dv_ref[...] = jnp.zeros_like(dv_ref)

    @pl.when(block == 0)
    def _():
        for shift, do_ref in enumerate(do_refs):
            rows = do_ref.shape[0]
            place = lax.rem(bounds[5, 0] + pieces - shift, pieces) * rows
            do_rows[pl.ds(pl.multiple_of(place, rows), rows), :] = do_ref[...]

    do = do_rows[pl.ds(pl.multiple_of(block * bq, bq), bq), :]
    q_of, do_of = halves(q_ref[...]), halves(do)
    product = do.astype(f32) * o_ref[...].astype(f32)
    high = product.astype(bf16)
    low = (product - high.astype(f32)).astype(bf16)
    row = lax.broadcasted_iota(jnp.int32, (8, LANES), 0)
    lane = lax.broadcasted_iota(jnp.int32, (8, LANES), 1)
    ones = jnp.where(lane // HEAD == row, 1.0, 0.0).astype(bf16)
    delta = dot(ones, high, contract_last) + dot(ones, low, contract_last)

    def step(masked, j, accs):
        at = pl.multiple_of(j * bk, bk)
        here = pl.ds(at, bk)
        if masked:
            ok = allowed_keys(at, bounds[0, block], low_ref[:1, :], bk, bq)
        k, v = k_ref[0, here, :], v_ref[0, here, :]
        scores = [dot(k, q_of[h], contract_last) for h in range(2)]
        d_probs = [dot(v, do_of[h], contract_last) for h in range(2)]
        dk, dv, new = [], [], []
        for h in range(2):
            p = jnp.exp(scores[h] - lse_ref[0, h : h + 1, :])
            if masked:
                p = jnp.where(ok, p, 0.0)
            ds = (p * (d_probs[h] - delta[h : h + 1, :])).astype(bf16)
            dv.append(dot(p.astype(bf16), do_of[h]))
            dk.append(dot(ds, q_of[h]))
            new.append(accs[h] + dot(kt_ref[:, here], ds))
        dk_ref[here, :] += dk[0] + dk[1]
        dv_ref[here, :] += dv[0] + dv[1]
        return tuple(new)

    accs = over_blocks(bounds, block, step, (jnp.zeros((HEAD, bq), f32),) * 2)
    g = jnp.concatenate(accs, 0).T
    dq_ref[...] = ((g * cos_ref[...] - swap_halves(g) * sin_ref[...]) * HEAD**-0.5).astype(bf16)


def attend_back(bounds, queries, attended, low, sums, cosine, sine, both, turned, d_attended, g, kv, bq, bk):
    rows, keys = queries.shape[0], both.shape[1]
    cols = queries.shape[1] // kv
    pairs, pieces = cols // LANES, len(d_attended)
    mine = pl.BlockSpec((bq, LANES), lambda p, i, b: (i, p))
    table = pl.BlockSpec((bq, LANES), lambda p, i, b: (i, 0))
    head = lambda at: pl.BlockSpec((1, keys, LANES), lambda p, i, b: (at, 0, 0))
    whole = pl.BlockSpec((keys, LANES), lambda p, i, b: (0, 0))
    size = rows * cols * keys
    return pl.pallas_call(
        functools.partial(attend_back_kernel, bq, bk, pieces),
        grid_spec=pltpu.PrefetchScalarGridSpec(
            num_scalar_prefetch=1, grid=(pairs, rows // bq),
            in_specs=[
                pl.BlockSpec((bq, LANES), lambda p, i, b: (i, g * pairs + p)), mine,
                pl.BlockSpec((8, bq), lambda p, i, b: (0, i)), pl.BlockSpec((1, 8, bq), lambda p, i, b: (p, 0, i)),
                table, table, head(g), pl.BlockSpec((HEAD, keys), lambda p, i, b: (g, 0)), head(kv + g),
            ] + [pl.BlockSpec((rows // pieces, LANES), lambda p, i, b: (0, g * pairs + p))] * pieces,
            out_specs=[mine, whole, whole],
            scratch_shapes=[pltpu.VMEM((rows, LANES), bf16)],
        ),
        out_shape=[jax.ShapeDtypeStruct((rows, cols), bf16)] + [jax.ShapeDtypeStruct((keys, LANES), f32)] * 2,
        compiler_params=pltpu.CompilerParams(vmem_limit_bytes=60 * 2**20),
        cost_estimate=pl.CostEstimate(flops=44 * size, bytes_accessed=8 * rows * cols, transcendentals=size // HEAD),
        name="attend_back",
    )(bounds, queries, attended, low, sums, cosine, sine, both, turned, both, *d_attended)


def block_bounds(starts, low, bq, bk, tp_me):
    low = low.reshape(-1, bq)
    begin, end = low[:, 0] // bk, (starts + bq + bk - 1) // bk
    whole = jnp.clip((low[:, -1] + bk - 1) // bk, begin, end)
    diagonal = jnp.clip((starts + 1) // bk, whole, end)
    return jnp.stack([starts, begin, whole, diagonal, end, jnp.full_like(starts, tp_me)]).astype(jnp.int32)


def ffn_kernel(tiles, earlier, x_ref, c_ref, gate_ref, up_ref, down_ref, *rest):
    act_ref, d_gate_ref, d_up_ref, out_ref, acc = rest[earlier:]
    tile = pl.program_id(0)
    x = x_ref[...]
    c = c_ref[...].reshape(x.shape)
    gate, up = dot(x, gate_ref[...]), dot(x, up_ref[...])
    d_act = dot(c, down_ref[...], contract_last)
    sig = 1.0 / (1.0 + jnp.exp(-gate))
    swish = gate * sig
    d_gate = (d_act * up * sig * (1.0 + gate * (1.0 - sig))).astype(bf16)
    d_up = (d_act * swish).astype(bf16)
    act_ref[...] = (swish * up).astype(bf16).reshape(act_ref.shape)
    d_gate_ref[...] = d_gate.reshape(act_ref.shape)
    d_up_ref[...] = d_up.reshape(act_ref.shape)
    part = dot(d_gate, gate_ref[...], contract_last) + dot(d_up, up_ref[...], contract_last)

    @pl.when(tile == 0)
    def _():
        acc[...] = part

    @pl.when(tile > 0)
    def _():
        acc[...] += part

    @pl.when(tile == tiles - 1)
    def _():
        out_ref[...] = acc[...].astype(bf16)


def ffn_chunk(x, c, gate_weight, up_weight, down_weight, chunk, earlier):
    rows, width = x.shape
    groups, own = c.shape[:2]
    hidden = gate_weight.shape[1]
    tn = min(512, hidden)
    tiles, part = hidden // tn, rows // groups
    column = pl.BlockSpec((width, tn), lambda j: (0, j))
    result = pl.BlockSpec((groups, part, tn), lambda j: (0, chunk, j))
    whole = pl.BlockSpec((rows, width), lambda j: (0, 0))
    return pl.pallas_call(
        functools.partial(ffn_kernel, tiles, len(earlier)),
        grid=(tiles,),
        in_specs=[
            whole, pl.BlockSpec((groups, part, width), lambda j: (0, chunk, 0)), column, column,
            pl.BlockSpec((tn, width), lambda j: (j, 0)),
        ] + [pl.BlockSpec(memory_space=pl.ANY)] * len(earlier),
        out_specs=[result] * 3 + [whole],
        scratch_shapes=[pltpu.VMEM((rows, width), f32)],
        out_shape=[jax.ShapeDtypeStruct((groups, own, hidden), bf16)] * 3
        + [jax.ShapeDtypeStruct((rows, width), bf16)],
        input_output_aliases={5 + i: i for i in range(len(earlier))},
        compiler_params=pltpu.CompilerParams(vmem_limit_bytes=60 * 2**20),
        cost_estimate=pl.CostEstimate(
            flops=16 * rows * width * hidden, bytes_accessed=6 * width * hidden, transcendentals=rows * hidden
        ),
        name="feed_forward",
    )(x, c, gate_weight, up_weight, down_weight, *earlier)


def branch_kernel(shifts, attended_ref, o_ref, x_ref, gain_ref, mid_ref, unit_ref, normed_ref, rstd_ref):
    shift = pl.program_id(0)
    o = o_ref[...].reshape(-1, mid_ref.shape[1])
    groups, wide = attended_ref.shape[1], attended_ref.shape[3]
    part = sum(dot(attended_ref[0, g], o[g * wide : (g + 1) * wide]) for g in range(groups))

    @pl.when(shift == 0)
    def _():
        mid_ref[...] = x_ref[...].astype(f32) + part

    @pl.when(shift > 0)
    def _():
        mid_ref[...] += part

    @pl.when(shift == shifts - 1)
    def _():
        mid = mid_ref[...]
        rstd = lax.rsqrt(jnp.mean(mid * mid, -1, keepdims=True) + epsilon)
        unit = mid * rstd
        unit_ref[...] = unit
        normed_ref[...] = (unit * gain_ref[...]).astype(bf16)
        rstd_ref[...] = jnp.broadcast_to(rstd, rstd_ref.shape)


def branch(attended, o, x, gain):
    shifts, groups, own, wide = attended.shape
    plane, _, rows, width = o.shape
    whole = lambda cols: pl.BlockSpec((own, cols), lambda d: (0, 0))
    shapes = [((own, width), f32), ((own, width), f32), ((own, width), bf16), ((own, LANES), f32)]
    return pl.pallas_call(
        functools.partial(branch_kernel, shifts),
        grid=(shifts,),
        in_specs=[
            pl.BlockSpec((1, groups, own, wide), lambda d: (d, 0, 0, 0)),
            pl.BlockSpec((plane, 1, rows, width), lambda d: (0, d, 0, 0)),
            whole(width), pl.BlockSpec((1, width), lambda d: (0, 0)),
        ],
        out_specs=[whole(shape[1]) for shape, _ in shapes],
        out_shape=[jax.ShapeDtypeStruct(*shape) for shape in shapes],
        compiler_params=pltpu.CompilerParams(vmem_limit_bytes=60 * 2**20),
        name="branch",
    )(attended, o, x, gain[None])


def branch_back_kernel(x_ref, o_ref, out_ref):
    out_ref[0] = dot(x_ref[...], o_ref[...].reshape(-1, x_ref.shape[1]), contract_last).astype(bf16)


def branch_back(x, o):
    plane, shifts, rows, width = o.shape
    own = x.shape[0]
    return pl.pallas_call(
        branch_back_kernel,
        grid=(shifts,),
        in_specs=[
            pl.BlockSpec((own, width), lambda d: (0, 0)),
            pl.BlockSpec((plane, 1, rows, width), lambda d: (0, lax.rem(shifts - d, shifts), 0, 0)),
        ],
        out_specs=pl.BlockSpec((1, own, plane * rows), lambda d: (d, 0, 0)),
        out_shape=jax.ShapeDtypeStruct((shifts, own, plane * rows), bf16),
        compiler_params=pltpu.CompilerParams(vmem_limit_bytes=60 * 2**20),
        name="branch_back",
    )(x, o)


def bits_of(n):
    return [1 << b for b in range(n.bit_length() - 1)]


def exchange(x, axis, bit):
    n = lax.axis_size(axis)
    return lax.ppermute(x, axis, [(i, i ^ bit) for i in range(n)])


def gather_ctx(x):
    n = lax.axis_size("ctx")
    held = {0: x}
    for bit in reversed(bits_of(n)):
        held.update({mask ^ bit: exchange(piece, "ctx", bit) for mask, piece in held.items()})
    return [held[mask] for mask in range(n)]


def scatter_sum_ctx(x):
    n, me = lax.axis_size("ctx"), lax.axis_index("ctx")
    x = x.reshape(n, -1, x.shape[1])
    for bit in bits_of(n):
        x = x.reshape(-1, 2, *x.shape[1:])
        mine = (me // bit) % 2
        send = lax.dynamic_index_in_dim(x, 1 - mine, 1, False)
        keep = lax.dynamic_index_in_dim(x, mine, 1, False)
        x = (keep.astype(f32) + exchange(send, "ctx", bit).astype(f32)).astype(bf16)
    return x[0]


def mirror_ctx(x):
    n = lax.axis_size("ctx")
    return lax.ppermute(x, "ctx", [(i, n - 1 - i) for i in range(n)])


def home_pairs(n_ctx, n_tp, shift):
    pairs = []
    for c in range(n_ctx):
        for t in range(n_tp):
            to = (t + shift) % n_tp
            pairs.append((c * n_tp + t, (c if to < n_tp // 2 else n_ctx - 1 - c) * n_tp + to))
    return pairs


def to_tokens(x):
    n, me = lax.axis_size("tp"), lax.axis_index("tp")
    x = x.reshape(n, -1, x.shape[1])
    out = []
    for d in range(n):
        piece = lax.dynamic_index_in_dim(x, (me + d) % n, 0, False)
        out.append(lax.ppermute(piece, ("ctx", "tp"), home_pairs(lax.axis_size("ctx"), n, d)))
    return out


def to_heads(pieces):
    n, n_ctx = lax.axis_size("tp"), lax.axis_size("ctx")
    out = []
    for d, piece in enumerate(pieces):
        pairs = [(to, at) for at, to in home_pairs(n_ctx, n, (n - d) % n)]
        out.append(lax.ppermute(piece, ("ctx", "tp"), pairs))
    return out


def shift_tp(x, d):
    n = lax.axis_size("tp")
    return lax.ppermute(x, "tp", [(i, (i + d) % n) for i in range(n)]) if d else x


def gather_direct(x):
    n, me = lax.axis_size("tp"), lax.axis_index("tp")
    pieces = jnp.stack([shift_tp(x, d) for d in range(n)])
    return jnp.concatenate([lax.dynamic_index_in_dim(pieces, (me - t) % n, 0, False) for t in range(n)], 0)


def scatter_direct(x):
    n, me = lax.axis_size("tp"), lax.axis_index("tp")
    x = x.reshape(n, -1, x.shape[1])
    return sum(shift_tp(lax.dynamic_index_in_dim(x, (me + d) % n, 0, False), d).astype(f32) for d in range(n))


def share_rows(weight):
    n, plane = lax.axis_size("tp"), lax.axis_size("dp") * lax.axis_size("ctx")
    at = lax.axis_index("dp") * lax.axis_size("ctx") + lax.axis_index("ctx")
    share = lax.dynamic_index_in_dim(weight.reshape(plane, -1, weight.shape[1]), at, 0, False)
    return jnp.concatenate([shift_tp(share, d) for d in range(n)], 0)


def gather_shares(shares):
    n = lax.axis_size("tp")
    whole = lax.all_gather(shares, ("dp", "ctx"), axis=0, tiled=True)
    return whole.reshape(-1, n, shares.shape[0] // n, shares.shape[1])


def halve(x, mine, send):
    x = x.reshape(2, -1, x.shape[1])
    keep = lax.dynamic_index_in_dim(x, mine, 0, False)
    other = lax.dynamic_index_in_dim(x, 1 - mine, 0, False)
    return (keep.astype(f32) + send(other).astype(f32)).astype(bf16)


def double(x, mine, send):
    other = send(x)
    return jnp.where(mine == 0, jnp.concatenate([x, other], 0), jnp.concatenate([other, x], 0))


def plane_stages():
    def step(axis, bit):
        return (lax.axis_index(axis) // bit) % 2, lambda piece: exchange(piece, axis, bit)

    near, *far = [step("ctx", bit) for bit in bits_of(lax.axis_size("ctx"))]
    across = [step("dp", bit) for bit in bits_of(lax.axis_size("dp"))]
    orders = (far + across, across + far)

    def first(parts):
        x = halve(parts[0], *near)
        return list(x.reshape(2, -1, x.shape[1]))

    def last(parts):
        mine, send = near
        others = [send(part) for part in parts]
        order = jnp.where(mine == 0, jnp.concatenate(parts + others, 0), jnp.concatenate(others + parts, 0))
        return [order.astype(f32)]

    def each(move, k):
        return lambda parts: [move(part, *order[k]) for part, order in zip(parts, orders)]

    steps = range(len(orders[0]))
    return [first] + [each(halve, k) for k in steps] + [each(double, k) for k in reversed(steps)] + [last]


class Sums:
    def __init__(self):
        self.stages, self.at, self.parts = plane_stages(), {}, {}

    def begin(self, name, x):
        self.at[name], self.parts[name] = 0, [x]

    def move(self, **steps):
        for name, count in steps.items():
            for _ in range(min(count, len(self.stages) - self.at[name])):
                self.parts[name] = self.stages[self.at[name]](self.parts[name])
                self.at[name] += 1

    def meet(self, values):
        values, self.parts = barrier((values, self.parts))
        return values

    def end(self, name):
        self.move(**{name: len(self.stages)})
        return self.parts[name][0]


def sum_all(x):
    for axis in ("ctx", "tp", "dp"):
        for bit in bits_of(lax.axis_size(axis)):
            x = x + exchange(x, axis, bit)
    return x


def norm_back(grad, unit, inverse_root, gain):
    scaled = grad * gain
    return inverse_root * (scaled - unit * jnp.mean(scaled * unit, -1, keepdims=True))


def gather_tp(x):
    return lax.all_gather(x, "tp", axis=0, tiled=True)


def scatter_tp(x):
    return lax.psum_scatter(x, "tp", scatter_dimension=0, tiled=True)


def on_device(
    tokens, lengths, q_weight, k_weight, v_weight, o_weight, gate_weight, up_weight, down_weight,
    attention_gain, ffn_gain, cotangent,
):
    ctx, me = lax.axis_size("ctx"), lax.axis_index("ctx")
    own = tokens.shape[1]
    block = own * lax.axis_size("tp")
    half = block // 2
    q_cols, kv_cols = q_weight.shape[1], k_weight.shape[1]
    kv = kv_cols // HEAD

    x = tokens[0].astype(f32)
    rstd1 = lax.rsqrt(jnp.mean(x * x, -1, keepdims=True) + epsilon)
    unit1 = x * rstd1
    normed = gather_tp((unit1 * attention_gain).astype(bf16))
    o_shares = share_rows(o_weight)
    w_kv = jnp.concatenate([k_weight, v_weight], 1)

    index = me * block + jnp.arange(block, dtype=jnp.int32)
    cosine, sine = rope_tables(index - doc_starts(lengths[0], index))
    far = (2 * ctx - 1 - 2 * me) * half
    near = me * block
    steps = jnp.arange(half, dtype=jnp.int32)
    q_index = jnp.concatenate([near + steps, far + steps])
    q_low = doc_starts(lengths[0], q_index)
    q_cos, q_sin = rope_tables(q_index - q_low)
    bq = bk = min(512, half)
    bounds = block_bounds(q_index.reshape(-1, bq)[:, 0], q_low, bq, bk, lax.axis_index("tp"))
    low_rows = jnp.broadcast_to(q_low[None, :], (8, block))
    normed, w_kv, cosine, sine, q_cos, q_sin, bounds, low_rows = barrier(
        (normed, w_kv, cosine, sine, q_cos, q_sin, bounds, low_rows)
    )
    kv_own = project(normed, w_kv, cosine, sine, 0, kv_cols)
    kv_all = gather_ctx(kv_own)
    q_own = project(normed, q_weight, cosine, sine, q_cols, q_cols)
    queries = jnp.concatenate([q_own[:half], mirror_ctx(q_own[half:])], 0)
    c_own, _ = barrier((cotangent[0], normed))
    queries, kv_all, o_shares = barrier((queries, kv_all, o_shares))
    both, turned = spread(me[None], kv_all, kv)
    o_full = gather_shares(o_shares)
    c_full = gather_direct(c_own)
    parts = [attend(bounds, queries, low_rows, both, turned, g, kv, bq, bk) for g in range(kv)]
    sent = [to_tokens(attended) for attended, _ in parts]
    attended_own = jnp.stack([jnp.stack(pieces) for pieces in zip(*sent)])
    attended_own, c_full = barrier((attended_own, c_full))
    attended_z = jnp.concatenate([attended for attended, _ in parts], 1)
    attended = jnp.concatenate([attended_z[:half], mirror_ctx(attended_z[half:])], 0)

    mid, unit2, ffn_own, rstd2 = branch(attended_own, o_full, tokens[0], ffn_gain)
    rstd2 = rstd2[:, :1]
    part = own // CHUNKS
    tp = lax.axis_size("tp")
    c_rows = c_full.reshape(tp, own, -1)
    gathered, hidden, scattered = [], [], []
    for chunk in range(CHUNKS):
        piece = ffn_own[chunk * part : (chunk + 1) * part]
        if gathered:
            piece, _ = barrier((piece, gathered[-1]))
        gathered.append(gather_tp(piece))
    for chunk in range(CHUNKS):
        *hidden, out = ffn_chunk(gathered[chunk], c_rows, gate_weight, up_weight, down_weight, chunk, hidden)
        if scattered:
            out, _ = barrier((out, scattered[-1]))
        scattered.append(scatter_tp(out))
    act, d_gate, d_up = [h.reshape(block, -1) for h in hidden]
    d_ffn = jnp.concatenate(scattered, 0).astype(f32)
    ffn_normed = jnp.stack([g.reshape(tp, part, -1) for g in gathered], 1).reshape(block, -1)

    d_mid = c_own.astype(f32) + norm_back(d_ffn, unit2, rstd2, ffn_gain)
    ffn_gain_part = jnp.sum(d_ffn * unit2, 0)
    d_branch = d_mid.astype(bf16)
    d_attended = to_heads(list(branch_back(d_branch, o_full)))
    d_branch, d_attended = barrier((d_branch, d_attended))
    d_branch = gather_tp(d_branch)
    out_part = dot(act, down_weight).astype(bf16)

    sums = Sums()
    sums.begin("gate", dot(ffn_normed, d_gate, contract_first).astype(bf16))
    sums.begin("up", dot(ffn_normed, d_up, contract_first).astype(bf16))
    sums.begin("down", dot(act, c_full, contract_first).astype(bf16))
    sums.move(gate=2, up=1, down=1)
    d_attended, out_part = sums.meet((d_attended, out_part))
    out_sum = scatter_tp(out_part)
    back = []
    for g in range(kv):
        if g:
            sums.move(gate=1, up=1, down=1)
            d_attended, back = sums.meet((d_attended, back))
        back.append(
            attend_back(
                bounds, queries, parts[g][0], low_rows, parts[g][1], q_cos, q_sin, both, turned, d_attended, g, kv, bq, bk
            )
        )
    sums.move(gate=1, up=1, down=1)
    back, d_branch = sums.meet((back, d_branch))
    sums.begin("o", dot(attended, d_branch, contract_first).astype(bf16))
    d_q = jnp.concatenate([dq for dq, _, _ in back], 1)
    d_q = jnp.concatenate([d_q[:half], mirror_ctx(d_q[half:])], 0)
    d_kv = jnp.concatenate([back[g][i][:, :HEAD] + back[g][i][:, HEAD:] for i in (1, 2) for g in range(kv)], 1)
    d_kv = rope(scatter_sum_ctx(d_kv.astype(bf16)), cosine, -sine, 0, kv_cols)
    sums.move(gate=1, up=1, down=1, o=1)
    d_q, d_kv = sums.meet((d_q, d_kv))
    d_normed_part = (dot(d_q, q_weight, contract_last) + dot(d_kv, w_kv, contract_last)).astype(bf16)
    d_normed_part, out_sum = barrier((d_normed_part, out_sum))
    d_normed = scatter_tp(d_normed_part).astype(f32)
    output = (mid + out_sum.astype(f32)).astype(bf16)[None]
    sums.begin("qkv", dot(normed, jnp.concatenate([d_q, d_kv], 1), contract_first).astype(bf16))

    input_gradient = (d_mid + norm_back(d_normed, unit1, rstd1, attention_gain)).astype(bf16)[None]
    attn_gain_part = jnp.sum(d_normed * unit1, 0)
    d_gains = sum_all(jnp.stack([attn_gain_part, ffn_gain_part]))
    d_qkv_w, d_o, d_gate_w, d_up_w, d_down = [sums.end(name) for name in ("qkv", "o", "gate", "up", "down")]
    d_q_w, d_kv_w = d_qkv_w[:, :q_cols], d_qkv_w[:, q_cols:]
    grads = (d_q_w, d_kv_w[:, :kv_cols], d_kv_w[:, kv_cols:], d_o, d_gate_w, d_up_w, d_down)
    return (output, input_gradient, *grads, d_gains[0], d_gains[1])


def solution(mesh):
    rows = P("dp", ("ctx", "tp"), None)
    columns, across = P(None, "tp"), P("tp", None)
    return jax.shard_map(
        on_device,
        mesh=mesh,
        in_specs=(
            rows, P("dp", None), columns, columns, columns, across, columns, columns, across, P(), P(), rows,
        ),
        out_specs=(rows, rows, columns, columns, columns, across, columns, columns, across, P(), P()),
        check_vma=False,
    )
```

```python
import functools
import math

import jax
import jax.numpy as jnp
from jax import lax
from jax.experimental import pallas as pl
from jax.experimental.pallas import tpu as pltpu
from jax.sharding import PartitionSpec as P

HEAD = 64
LANES = 128
epsilon = 1e-05
negative = -1e30
plain = (((1,), (0,)), ((), ()))
contract_first = (((0,), (0,)), ((), ()))
contract_last = (((1,), (1,)), ((), ()))
bf16 = jnp.bfloat16
f32 = jnp.float32
barrier = lax.optimization_barrier
CHUNKS = 2


def dot(left, right, dims=plain):
    return lax.dot_general(left, right, dims, preferred_element_type=f32)


def rope_tables(positions):
    half = HEAD // 2
    steps = jnp.arange(half, dtype=f32)
    base = jnp.power(f32(500000.0), -2.0 * steps / HEAD)
    wavelen = 2.0 * math.pi / base
    smooth = (8192.0 / wavelen - 1.0) / 3.0
    between = (1.0 - smooth) * base / 32.0 + smooth * base
    used = jnp.where(wavelen > 8192.0, base / 32.0, jnp.where(wavelen < 2048.0, base, between))
    angle = positions.astype(f32)[:, None] * jnp.tile(used, LANES // half)[None, :]
    sign = jnp.where(jnp.arange(LANES) % HEAD < half, -1.0, 1.0).astype(f32)
    return jnp.cos(angle), jnp.sin(angle) * sign[None, :]


def doc_starts(lengths_row, index):
    count = lengths_row.shape[0]
    docs = jnp.arange(count, dtype=jnp.int32)
    ends = jnp.sum(jnp.where(docs[None, :] <= docs[:, None], lengths_row[None, :], 0), 1)
    return jnp.max(jnp.where(index[:, None] >= ends[None, :], ends[None, :], 0), 1)


def swap_halves(v):
    lane = lax.broadcasted_iota(jnp.int32, v.shape, 1)
    return jnp.where(lane % HEAD < HEAD // 2, pltpu.roll(v, LANES - HEAD // 2, 1), pltpu.roll(v, HEAD // 2, 1))


def rope_kernel(q_cols, turned, x_ref, cos_ref, sin_ref, out_ref):
    cosine, sine = cos_ref[...], sin_ref[...]
    lane = lax.broadcasted_iota(jnp.int32, cosine.shape, 1)
    for at in range(0, x_ref.shape[1], LANES):
        v = x_ref[:, at : at + LANES].astype(f32)
        if at < turned:
            r = v * cosine + swap_halves(v) * sine
            v = r if at + LANES <= turned else jnp.where(lane < turned - at, r, v)
            if at < q_cols:
                v = v * HEAD**-0.5
        out_ref[:, at : at + LANES] = v.astype(bf16)


def rope(x, cosine, sine, q_cols, turned):
    rows, cols = x.shape
    step = min(rows, 256)
    return pl.pallas_call(
        functools.partial(rope_kernel, q_cols, turned),
        grid=(rows // step,),
        in_specs=[
            pl.BlockSpec((step, cols), lambda i: (i, 0)),
            pl.BlockSpec((step, LANES), lambda i: (i, 0)),
            pl.BlockSpec((step, LANES), lambda i: (i, 0)),
        ],
        out_specs=pl.BlockSpec((step, cols), lambda i: (i, 0)),
        out_shape=jax.ShapeDtypeStruct((rows, cols), bf16),
        name="rotate",
    )(x, cosine, sine)


def project_kernel(q_cols, turned, x_ref, w_ref, cos_ref, sin_ref, out_ref, sums):
    sums[...] = dot(x_ref[...], w_ref[...])
    rope_kernel(q_cols, turned, sums, cos_ref, sin_ref, out_ref)


def project(x, w, cosine, sine, q_cols, turned):
    rows, depth = x.shape
    cols = w.shape[1]
    step = min(rows, 256)
    return pl.pallas_call(
        functools.partial(project_kernel, q_cols, turned),
        grid=(rows // step,),
        in_specs=[
            pl.BlockSpec((step, depth), lambda i: (i, 0)),
            pl.BlockSpec((depth, cols), lambda i: (0, 0)),
            pl.BlockSpec((step, LANES), lambda i: (i, 0)),
            pl.BlockSpec((step, LANES), lambda i: (i, 0)),
        ],
        out_specs=pl.BlockSpec((step, cols), lambda i: (i, 0)),
        out_shape=jax.ShapeDtypeStruct((rows, cols), bf16),
        scratch_shapes=[pltpu.VMEM((step, cols), f32)],
        compiler_params=pltpu.CompilerParams(vmem_limit_bytes=40 * 2**20),
        cost_estimate=pl.CostEstimate(flops=2 * rows * depth * cols, bytes_accessed=2 * rows * depth, transcendentals=0),
        name="project",
    )(x, w, cosine, sine)


def spread_kernel(kv, n, here, *refs):
    pieces, (both_ref, turned_ref) = refs[:n], refs[n:]
    for mask, piece in enumerate(pieces):
        rows = piece.shape[0]
        place = pl.ds(pl.multiple_of((here[0] ^ mask) * rows, rows), rows)
        for at in range(0, piece.shape[1], LANES):
            x = piece[:, at : at + LANES].astype(f32)
            other = pltpu.roll(x, HEAD, 1)
            left = lax.broadcasted_iota(jnp.int32, x.shape, 1) < HEAD
            head = at // HEAD
            both_ref[head, place, :] = jnp.where(left, x, other).astype(bf16)
            both_ref[head + 1, place, :] = jnp.where(left, other, x).astype(bf16)
            turned_ref[at : at + LANES, place] = x.T.astype(bf16)


def spread(here, pieces, kv):
    n, (rows, cols) = len(pieces), pieces[0].shape
    return pl.pallas_call(
        functools.partial(spread_kernel, kv, n),
        grid_spec=pltpu.PrefetchScalarGridSpec(
            num_scalar_prefetch=1, grid=(1,),
            in_specs=[pl.BlockSpec((rows, cols), lambda i, h: (0, 0))] * n,
            out_specs=[
                pl.BlockSpec((2 * kv, n * rows, LANES), lambda i, h: (0, 0, 0)),
                pl.BlockSpec((cols, n * rows), lambda i, h: (0, 0)),
            ],
        ),
        out_shape=[
            jax.ShapeDtypeStruct((2 * kv, n * rows, LANES), bf16),
            jax.ShapeDtypeStruct((cols, n * rows), bf16),
        ],
        compiler_params=pltpu.CompilerParams(vmem_limit_bytes=60 * 2**20),
        name="spread",
    )(here, *pieces)


def over_blocks(bounds, block, step, carry):
    b0, b1, b2, b3 = [bounds[1 + k, block] for k in range(4)]
    carry = lax.fori_loop(b0, b1, functools.partial(step, True), carry)
    carry = lax.fori_loop(b1, b2, functools.partial(step, False), carry)
    return lax.fori_loop(b2, b3, functools.partial(step, True), carry)


def allowed_keys(at, first_row, low, bk, bq):
    key = at + lax.broadcasted_iota(jnp.int32, (bk, bq), 0)
    row = first_row + lax.broadcasted_iota(jnp.int32, (bk, bq), 1)
    return (key <= row) & (key >= low)


def halves(x):
    left = lax.broadcasted_iota(jnp.int32, x.shape, 1) < HEAD
    zero = jnp.zeros_like(x)
    return [jnp.where(left, x, zero), jnp.where(left, zero, x)]


def attend_kernel(bq, bk, bounds, q_ref, low_ref, k_ref, vt_ref, o_ref, lse_ref):
    block = pl.program_id(0)
    pairs = q_ref.shape[1] // LANES
    heads = range(2 * pairs)
    q = sum([halves(q_ref[:, p * LANES : (p + 1) * LANES]) for p in range(pairs)], [])

    def step(masked, j, carry):
        peaks, totals, accs = carry
        at = pl.multiple_of(j * bk, bk)
        if masked:
            ok = allowed_keys(at, bounds[0, block], low_ref[:1, :], bk, bq)
        k = k_ref[0, pl.ds(at, bk), :]
        scores = [dot(k, q[h], contract_last) for h in heads]
        new_peaks, new_totals, new_accs = [], [], []
        for h in heads:
            s = scores[h]
            if masked:
                s = jnp.where(ok, s, negative)
            peak = jnp.maximum(peaks[h], jnp.max(s, 0, keepdims=True))
            p = jnp.exp(s - peak)
            if masked:
                p = jnp.where(ok, p, 0.0)
            decay = jnp.exp(peaks[h] - peak)
            new_peaks.append(peak)
            new_totals.append(totals[h] * decay + jnp.sum(p, 0, keepdims=True))
            new_accs.append(accs[h] * decay + dot(vt_ref[:, pl.ds(at, bk)], p.astype(bf16)))
        return tuple(new_peaks), tuple(new_totals), tuple(new_accs)

    start = [(jnp.full((1, bq), negative, f32),) * len(heads), (jnp.zeros((1, bq), f32),) * len(heads)]
    start.append((jnp.zeros((HEAD, bq), f32),) * len(heads))
    peaks, totals, accs = over_blocks(bounds, block, step, tuple(start))
    for p in range(pairs):
        pair = [accs[h] / totals[h] for h in (2 * p, 2 * p + 1)]
        o_ref[:, p * LANES : (p + 1) * LANES] = jnp.concatenate(pair, 0).T.astype(bf16)
    for h in heads:
        lse_ref[h // 2, h % 2 : h % 2 + 1, :] = peaks[h] + jnp.log(totals[h])


def attend(bounds, queries, low, both, turned, g, kv, bq, bk):
    rows, keys = queries.shape[0], both.shape[1]
    cols = queries.shape[1] // kv
    pairs = cols // LANES
    size = rows * cols * keys
    return pl.pallas_call(
        functools.partial(attend_kernel, bq, bk),
        grid_spec=pltpu.PrefetchScalarGridSpec(
            num_scalar_prefetch=1, grid=(rows // bq,),
            in_specs=[
                pl.BlockSpec((bq, cols), lambda i, b: (i, g)),
                pl.BlockSpec((8, bq), lambda i, b: (0, i)),
                pl.BlockSpec((1, keys, LANES), lambda i, b: (g, 0, 0)),
                pl.BlockSpec((HEAD, keys), lambda i, b: (kv + g, 0)),
            ],
            out_specs=[
                pl.BlockSpec((bq, cols), lambda i, b: (i, 0)),
                pl.BlockSpec((pairs, 8, bq), lambda i, b: (0, 0, i)),
            ],
        ),
        out_shape=[
            jax.ShapeDtypeStruct((rows, cols), bf16),
            jax.ShapeDtypeStruct((pairs, 8, rows), f32),
        ],
        compiler_params=pltpu.CompilerParams(vmem_limit_bytes=60 * 2**20),
        cost_estimate=pl.CostEstimate(flops=4 * size, bytes_accessed=8 * rows * cols, transcendentals=size // HEAD),
        name="attend",
    )(bounds, queries, low, both, turned)


def attend_back_kernel(
    bq, bk, pieces, bounds, q_ref, o_ref, low_ref, lse_ref, cos_ref, sin_ref, k_ref, kt_ref, v_ref, *rest
):
    do_refs, (dq_ref, dk_ref, dv_ref, do_rows) = rest[:pieces], rest[pieces:]
    pair, block = pl.program_id(0), pl.program_id(1)

    @pl.when((pair == 0) & (block == 0))
    def _():
        dk_ref[...] = jnp.zeros_like(dk_ref)
        dv_ref[...] = jnp.zeros_like(dv_ref)

    @pl.when(block == 0)
    def _():
        for shift, do_ref in enumerate(do_refs):
            rows = do_ref.shape[0]
            place = lax.rem(bounds[5, 0] + pieces - shift, pieces) * rows
            do_rows[pl.ds(pl.multiple_of(place, rows), rows), :] = do_ref[...]

    do = do_rows[pl.ds(pl.multiple_of(block * bq, bq), bq), :]
    q_of, do_of = halves(q_ref[...]), halves(do)
    product = do.astype(f32) * o_ref[...].astype(f32)
    high = product.astype(bf16)
    low = (product - high.astype(f32)).astype(bf16)
    row = lax.broadcasted_iota(jnp.int32, (8, LANES), 0)
    lane = lax.broadcasted_iota(jnp.int32, (8, LANES), 1)
    ones = jnp.where(lane // HEAD == row, 1.0, 0.0).astype(bf16)
    delta = dot(ones, high, contract_last) + dot(ones, low, contract_last)

    def step(masked, j, accs):
        at = pl.multiple_of(j * bk, bk)
        here = pl.ds(at, bk)
        if masked:
            ok = allowed_keys(at, bounds[0, block], low_ref[:1, :], bk, bq)
        k, v = k_ref[0, here, :], v_ref[0, here, :]
        scores = [dot(k, q_of[h], contract_last) for h in range(2)]
        d_probs = [dot(v, do_of[h], contract_last) for h in range(2)]
        dk, dv, new = [], [], []
        for h in range(2):
            p = jnp.exp(scores[h] - lse_ref[0, h : h + 1, :])
            if masked:
                p = jnp.where(ok, p, 0.0)
            ds = (p * (d_probs[h] - delta[h : h + 1, :])).astype(bf16)
            dv.append(dot(p.astype(bf16), do_of[h]))
            dk.append(dot(ds, q_of[h]))
            new.append(accs[h] + dot(kt_ref[:, here], ds))
        dk_ref[here, :] += dk[0] + dk[1]
        dv_ref[here, :] += dv[0] + dv[1]
        return tuple(new)

    accs = over_blocks(bounds, block, step, (jnp.zeros((HEAD, bq), f32),) * 2)
    g = jnp.concatenate(accs, 0).T
    dq_ref[...] = ((g * cos_ref[...] - swap_halves(g) * sin_ref[...]) * HEAD**-0.5).astype(bf16)


def attend_back(bounds, queries, attended, low, sums, cosine, sine, both, turned, d_attended, g, kv, bq, bk):
    rows, keys = queries.shape[0], both.shape[1]
    cols = queries.shape[1] // kv
    pairs, pieces = cols // LANES, len(d_attended)
    mine = pl.BlockSpec((bq, LANES), lambda p, i, b: (i, p))
    table = pl.BlockSpec((bq, LANES), lambda p, i, b: (i, 0))
    head = lambda at: pl.BlockSpec((1, keys, LANES), lambda p, i, b: (at, 0, 0))
    whole = pl.BlockSpec((keys, LANES), lambda p, i, b: (0, 0))
    size = rows * cols * keys
    return pl.pallas_call(
        functools.partial(attend_back_kernel, bq, bk, pieces),
        grid_spec=pltpu.PrefetchScalarGridSpec(
            num_scalar_prefetch=1, grid=(pairs, rows // bq),
            in_specs=[
                pl.BlockSpec((bq, LANES), lambda p, i, b: (i, g * pairs + p)), mine,
                pl.BlockSpec((8, bq), lambda p, i, b: (0, i)), pl.BlockSpec((1, 8, bq), lambda p, i, b: (p, 0, i)),
                table, table, head(g), pl.BlockSpec((HEAD, keys), lambda p, i, b: (g, 0)), head(kv + g),
            ] + [pl.BlockSpec((rows // pieces, LANES), lambda p, i, b: (0, g * pairs + p))] * pieces,
            out_specs=[mine, whole, whole],
            scratch_shapes=[pltpu.VMEM((rows, LANES), bf16)],
        ),
        out_shape=[jax.ShapeDtypeStruct((rows, cols), bf16)] + [jax.ShapeDtypeStruct((keys, LANES), f32)] * 2,
        compiler_params=pltpu.CompilerParams(vmem_limit_bytes=60 * 2**20),
        cost_estimate=pl.CostEstimate(flops=size, bytes_accessed=8 * rows * cols, transcendentals=size // HEAD),
        name="attend_back",
    )(bounds, queries, attended, low, sums, cosine, sine, both, turned, both, *d_attended)


def block_bounds(starts, low, bq, bk, tp_me):
    low = low.reshape(-1, bq)
    begin, end = low[:, 0] // bk, (starts + bq + bk - 1) // bk
    whole = jnp.clip((low[:, -1] + bk - 1) // bk, begin, end)
    diagonal = jnp.clip((starts + 1) // bk, whole, end)
    return jnp.stack([starts, begin, whole, diagonal, end, jnp.full_like(starts, tp_me)]).astype(jnp.int32)


def ffn_kernel(tiles, earlier, x_ref, c_ref, gate_ref, up_ref, down_ref, *rest):
    act_ref, d_gate_ref, d_up_ref, out_ref, acc = rest[earlier:]
    tile = pl.program_id(0)
    x = x_ref[...]
    c = c_ref[...].reshape(x.shape)
    gate, up = dot(x, gate_ref[...]), dot(x, up_ref[...])
    d_act = dot(c, down_ref[...], contract_last)
    sig = 1.0 / (1.0 + jnp.exp(-gate))
    swish = gate * sig
    d_gate = (d_act * up * sig * (1.0 + gate * (1.0 - sig))).astype(bf16)
    d_up = (d_act * swish).astype(bf16)
    act_ref[...] = (swish * up).astype(bf16).reshape(act_ref.shape)
    d_gate_ref[...] = d_gate.reshape(act_ref.shape)
    d_up_ref[...] = d_up.reshape(act_ref.shape)
    part = dot(d_gate, gate_ref[...], contract_last) + dot(d_up, up_ref[...], contract_last)

    @pl.when(tile == 0)
    def _():
        acc[...] = part

    @pl.when(tile > 0)
    def _():
        acc[...] += part

    @pl.when(tile == tiles - 1)
    def _():
        out_ref[...] = acc[...].astype(bf16)


def ffn_chunk(x, c, gate_weight, up_weight, down_weight, chunk, earlier):
    rows, width = x.shape
    groups, own = c.shape[:2]
    hidden = gate_weight.shape[1]
    tn = min(512, hidden)
    tiles, part = hidden // tn, rows // groups
    column = pl.BlockSpec((width, tn), lambda j: (0, j))
    result = pl.BlockSpec((groups, part, tn), lambda j: (0, chunk, j))
    whole = pl.BlockSpec((rows, width), lambda j: (0, 0))
    return pl.pallas_call(
        functools.partial(ffn_kernel, tiles, len(earlier)),
        grid=(tiles,),
        in_specs=[
            whole, pl.BlockSpec((groups, part, width), lambda j: (0, chunk, 0)), column, column,
            pl.BlockSpec((tn, width), lambda j: (j, 0)),
        ] + [pl.BlockSpec(memory_space=pl.ANY)] * len(earlier),
        out_specs=[result] * 3 + [whole],
        scratch_shapes=[pltpu.VMEM((rows, width), f32)],
        out_shape=[jax.ShapeDtypeStruct((groups, own, hidden), bf16)] * 3
        + [jax.ShapeDtypeStruct((rows, width), bf16)],
        input_output_aliases={5 + i: i for i in range(len(earlier))},
        compiler_params=pltpu.CompilerParams(vmem_limit_bytes=60 * 2**20),
        cost_estimate=pl.CostEstimate(
            flops=16 * rows * width * hidden, bytes_accessed=6 * width * hidden, transcendentals=rows * hidden
        ),
        name="feed_forward",
    )(x, c, gate_weight, up_weight, down_weight, *earlier)


def branch_kernel(shifts, attended_ref, o_ref, x_ref, gain_ref, mid_ref, unit_ref, normed_ref, rstd_ref):
    shift = pl.program_id(0)
    o = o_ref[...].reshape(-1, mid_ref.shape[1])
    groups, wide = attended_ref.shape[1], attended_ref.shape[3]
    part = sum(dot(attended_ref[0, g], o[g * wide : (g + 1) * wide]) for g in range(groups))

    @pl.when(shift == 0)
    def _():
        mid_ref[...] = x_ref[...].astype(f32) + part

    @pl.when(shift > 0)
    def _():
        mid_ref[...] += part

    @pl.when(shift == shifts - 1)
    def _():
        mid = mid_ref[...]
        rstd = lax.rsqrt(jnp.mean(mid * mid, -1, keepdims=True) + epsilon)
        unit = mid * rstd
        unit_ref[...] = unit
        normed_ref[...] = (unit * gain_ref[...]).astype(bf16)
        rstd_ref[...] = jnp.broadcast_to(rstd, rstd_ref.shape)


def branch(attended, o, x, gain):
    shifts, groups, own, wide = attended.shape
    plane, _, rows, width = o.shape
    whole = lambda cols: pl.BlockSpec((own, cols), lambda d: (0, 0))
    shapes = [((own, width), f32), ((own, width), f32), ((own, width), bf16), ((own, LANES), f32)]
    return pl.pallas_call(
        functools.partial(branch_kernel, shifts),
        grid=(shifts,),
        in_specs=[
            pl.BlockSpec((1, groups, own, wide), lambda d: (d, 0, 0, 0)),
            pl.BlockSpec((plane, 1, rows, width), lambda d: (0, d, 0, 0)),
            whole(width), pl.BlockSpec((1, width), lambda d: (0, 0)),
        ],
        out_specs=[whole(shape[1]) for shape, _ in shapes],
        out_shape=[jax.ShapeDtypeStruct(*shape) for shape in shapes],
        compiler_params=pltpu.CompilerParams(vmem_limit_bytes=60 * 2**20),
        name="branch",
    )(attended, o, x, gain[None])


def branch_back_kernel(x_ref, o_ref, out_ref):
    out_ref[0] = dot(x_ref[...], o_ref[...].reshape(-1, x_ref.shape[1]), contract_last).astype(bf16)


def branch_back(x, o):
    plane, shifts, rows, width = o.shape
    own = x.shape[0]
    return pl.pallas_call(
        branch_back_kernel,
        grid=(shifts,),
        in_specs=[
            pl.BlockSpec((own, width), lambda d: (0, 0)),
            pl.BlockSpec((plane, 1, rows, width), lambda d: (0, lax.rem(shifts - d, shifts), 0, 0)),
        ],
        out_specs=pl.BlockSpec((1, own, plane * rows), lambda d: (d, 0, 0)),
        out_shape=jax.ShapeDtypeStruct((shifts, own, plane * rows), bf16),
        compiler_params=pltpu.CompilerParams(vmem_limit_bytes=60 * 2**20),
        name="branch_back",
    )(x, o)


def bits_of(n):
    return [1 << b for b in range(n.bit_length() - 1)]


def exchange(x, axis, bit):
    n = lax.axis_size(axis)
    return lax.ppermute(x, axis, [(i, i ^ bit) for i in range(n)])


def gather_ctx(x):
    n = lax.axis_size("ctx")
    held = {0: x}
    for bit in reversed(bits_of(n)):
        held.update({mask ^ bit: exchange(piece, "ctx", bit) for mask, piece in held.items()})
    return [held[mask] for mask in range(n)]


def scatter_sum_ctx(x):
    n, me = lax.axis_size("ctx"), lax.axis_index("ctx")
    x = x.reshape(n, -1, x.shape[1])
    for bit in bits_of(n):
        x = x.reshape(-1, 2, *x.shape[1:])
        mine = (me // bit) % 2
        send = lax.dynamic_index_in_dim(x, 1 - mine, 1, False)
        keep = lax.dynamic_index_in_dim(x, mine, 1, False)
        x = (keep.astype(f32) + exchange(send, "ctx", bit).astype(f32)).astype(bf16)
    return x[0]


def mirror_ctx(x):
    n = lax.axis_size("ctx")
    return lax.ppermute(x, "ctx", [(i, n - 1 - i) for i in range(n)])


def home_pairs(n_ctx, n_tp, shift):
    pairs = []
    for c in range(n_ctx):
        for t in range(n_tp):
            to = (t + shift) % n_tp
            pairs.append((c * n_tp + t, (c if to < n_tp // 2 else n_ctx - 1 - c) * n_tp + to))
    return pairs


def to_tokens(x):
    n, me = lax.axis_size("tp"), lax.axis_index("tp")
    x = x.reshape(n, -1, x.shape[1])
    out = []
    for d in range(n):
        piece = lax.dynamic_index_in_dim(x, (me + d) % n, 0, False)
        out.append(lax.ppermute(piece, ("ctx", "tp"), home_pairs(lax.axis_size("ctx"), n, d)))
    return out


def to_heads(pieces):
    n, n_ctx = lax.axis_size("tp"), lax.axis_size("ctx")
    out = []
    for d, piece in enumerate(pieces):
        pairs = [(to, at) for at, to in home_pairs(n_ctx, n, (n - d) % n)]
        out.append(lax.ppermute(piece, ("ctx", "tp"), pairs))
    return out


def shift_tp(x, d):
    n = lax.axis_size("tp")
    return lax.ppermute(x, "tp", [(i, (i + d) % n) for i in range(n)]) if d else x


def in_order(pieces):
    n, me = lax.axis_size("tp"), lax.axis_index("tp")
    pieces = jnp.stack(pieces)
    return jnp.concatenate([lax.dynamic_index_in_dim(pieces, (me - t) % n, 0, False) for t in range(n)], 0)


def scatter_direct(x):
    n, me = lax.axis_size("tp"), lax.axis_index("tp")
    x = x.reshape(n, -1, x.shape[1])
    return sum(shift_tp(lax.dynamic_index_in_dim(x, (me + d) % n, 0, False), d).astype(f32) for d in range(n))


def gather_direct(x):
    return in_order([shift_tp(x, d) for d in range(lax.axis_size("tp"))])


def share_rows(weight):
    n, plane = lax.axis_size("tp"), lax.axis_size("dp") * lax.axis_size("ctx")
    at = lax.axis_index("dp") * lax.axis_size("ctx") + lax.axis_index("ctx")
    share = lax.dynamic_index_in_dim(weight.reshape(plane, -1, weight.shape[1]), at, 0, False)
    return jnp.concatenate([shift_tp(share, d) for d in range(n)], 0)


def gather_shares(shares):
    n = lax.axis_size("tp")
    whole = lax.all_gather(shares, ("dp", "ctx"), axis=0, tiled=True)
    return whole.reshape(-1, n, shares.shape[0] // n, shares.shape[1])


PLANE = ("dp", "ctx")


def sum_plane(*xs):
    return lax.psum(xs, PLANE)


def sum_all(x):
    for axis in ("ctx", "tp", "dp"):
        for bit in bits_of(lax.axis_size(axis)):
            x = x + exchange(x, axis, bit)
    return x


def norm_back(grad, unit, inverse_root, gain):
    scaled = grad * gain
    return inverse_root * (scaled - unit * jnp.mean(scaled * unit, -1, keepdims=True))


def gather_tp(x):
    return lax.all_gather(x, "tp", axis=0, tiled=True)


def scatter_tp(x):
    return lax.psum_scatter(x, "tp", scatter_dimension=0, tiled=True)


def on_device(
    tokens, lengths, q_weight, k_weight, v_weight, o_weight, gate_weight, up_weight, down_weight,
    attention_gain, ffn_gain, cotangent,
):
    ctx, me = lax.axis_size("ctx"), lax.axis_index("ctx")
    own = tokens.shape[1]
    block = own * lax.axis_size("tp")
    half = block // 2
    q_cols, kv_cols = q_weight.shape[1], k_weight.shape[1]
    kv = kv_cols // HEAD

    x = tokens[0].astype(f32)
    rstd1 = lax.rsqrt(jnp.mean(x * x, -1, keepdims=True) + epsilon)
    unit1 = x * rstd1
    normed = gather_tp((unit1 * attention_gain).astype(bf16))
    o_shares = share_rows(o_weight)
    w_kv = jnp.concatenate([k_weight, v_weight], 1)

    index = me * block + jnp.arange(block, dtype=jnp.int32)
    cosine, sine = rope_tables(index - doc_starts(lengths[0], index))
    far = (2 * ctx - 1 - 2 * me) * half
    near = me * block
    steps = jnp.arange(half, dtype=jnp.int32)
    q_index = jnp.concatenate([near + steps, far + steps])
    q_low = doc_starts(lengths[0], q_index)
    q_cos, q_sin = rope_tables(q_index - q_low)
    bq = bk = min(512, half)
    bounds = block_bounds(q_index.reshape(-1, bq)[:, 0], q_low, bq, bk, lax.axis_index("tp"))
    low_rows = jnp.broadcast_to(q_low[None, :], (8, block))
    normed, w_kv, cosine, sine, q_cos, q_sin, bounds, low_rows = barrier(
        (normed, w_kv, cosine, sine, q_cos, q_sin, bounds, low_rows)
    )
    kv_own = project(normed, w_kv, cosine, sine, 0, kv_cols)
    kv_all = gather_ctx(kv_own)
    q_own = project(normed, q_weight, cosine, sine, q_cols, q_cols)
    queries = jnp.concatenate([q_own[:half], mirror_ctx(q_own[half:])], 0)
    c_own, _ = barrier((cotangent[0], normed))
    queries, kv_all, o_shares = barrier((queries, kv_all, o_shares))
    both, turned = spread(me[None], kv_all, kv)
    o_full = gather_shares(o_shares)
    c_shifts = [shift_tp(c_own, d) for d in range(lax.axis_size("tp"))]
    parts = [attend(bounds, queries, low_rows, both, turned, g, kv, bq, bk) for g in range(kv)]
    sent = [to_tokens(attended) for attended, _ in parts]
    attended_own = jnp.stack([jnp.stack(pieces) for pieces in zip(*sent)])
    attended_own, c_shifts = barrier((attended_own, c_shifts))
    c_full = in_order(c_shifts)
    attended_z = jnp.concatenate([attended for attended, _ in parts], 1)
    attended = jnp.concatenate([attended_z[:half], mirror_ctx(attended_z[half:])], 0)

    mid, unit2, ffn_own, rstd2 = branch(attended_own, o_full, tokens[0], ffn_gain)
    rstd2 = rstd2[:, :1]
    part = own // CHUNKS
    tp = lax.axis_size("tp")
    c_rows = c_full.reshape(tp, own, -1)
    gathered, hidden, scattered = [], [], []
    for chunk in range(CHUNKS):
        piece = ffn_own[chunk * part : (chunk + 1) * part]
        if gathered:
            piece, _ = barrier((piece, gathered[-1]))
        gathered.append(gather_tp(piece))
    for chunk in range(CHUNKS):
        *hidden, out = ffn_chunk(gathered[chunk], c_rows, gate_weight, up_weight, down_weight, chunk, hidden)
        scattered.append(scatter_direct(out) if chunk == CHUNKS - 1 else scatter_tp(out).astype(f32))
    act, d_gate, d_up = [h.reshape(block, -1) for h in hidden]
    d_ffn = jnp.concatenate(scattered, 0)
    ffn_normed = jnp.stack([g.reshape(tp, part, -1) for g in gathered], 1).reshape(block, -1)

    d_mid = c_own.astype(f32) + norm_back(d_ffn, unit2, rstd2, ffn_gain)
    ffn_gain_part = jnp.sum(d_ffn * unit2, 0)
    d_gate_w = dot(ffn_normed, d_gate, contract_first).astype(bf16)
    d_up_w = dot(ffn_normed, d_up, contract_first).astype(bf16)
    d_branch, _ = barrier((d_mid.astype(bf16), (d_gate_w, d_up_w)))
    d_gate_w, d_up_w = sum_plane(d_gate_w, d_up_w)
    d_attended = to_heads(list(branch_back(d_branch, o_full)))
    d_branch, d_attended = barrier((d_branch, d_attended))
    d_branch = gather_direct(d_branch)
    d_down = dot(act, c_full, contract_first).astype(bf16)

    act_late, _ = barrier((act, d_branch))
    out_sum = scatter_direct(dot(act_late, down_weight).astype(bf16))

    d_o = dot(attended, d_branch, contract_first).astype(bf16)
    back = [
        attend_back(
            bounds, queries, parts[g][0], low_rows, parts[g][1], q_cos, q_sin, both, turned, d_attended, g, kv, bq, bk
        )
        for g in range(kv)
    ]
    d_q = jnp.concatenate([dq for dq, _, _ in back], 1)
    d_q = jnp.concatenate([d_q[:half], mirror_ctx(d_q[half:])], 0)
    d_kv = jnp.concatenate([back[g][i][:, :HEAD] + back[g][i][:, HEAD:] for i in (1, 2) for g in range(kv)], 1)
    d_kv = rope(scatter_sum_ctx(d_kv.astype(bf16)), cosine, -sine, 0, kv_cols)
    d_normed_part = dot(d_q, q_weight, contract_last) + dot(d_kv, w_kv, contract_last)
    d_normed_part, out_sum = barrier((d_normed_part.astype(bf16), out_sum))
    d_normed = scatter_direct(d_normed_part)
    d_qkv_w = dot(normed, jnp.concatenate([d_q, d_kv], 1), contract_first).astype(bf16)
    d_qkv_w, d_o, d_down, _ = barrier((d_qkv_w, d_o, d_down, (d_gate_w, d_up_w)))
    d_gate_w, d_up_w = d_gate_w.astype(f32), d_up_w.astype(f32)
    d_qkv_w, d_o, d_down = sum_plane(d_qkv_w, d_o, d_down)

    out_sum, _ = barrier((out_sum, (d_gate_w, d_up_w)))
    output = (mid + out_sum).astype(bf16)[None]
    d_normed, _ = barrier((d_normed, output))
    input_gradient = (d_mid + norm_back(d_normed, unit1, rstd1, attention_gain)).astype(bf16)[None]
    attn_gain_part = jnp.sum(d_normed * unit1, 0)
    d_gains = sum_all(jnp.stack([attn_gain_part, ffn_gain_part]))
    d_q_w, d_kv_w = d_qkv_w[:, :q_cols], d_qkv_w[:, q_cols:]
    grads = [
        g.astype(f32)
        for g in (d_q_w, d_kv_w[:, :kv_cols], d_kv_w[:, kv_cols:], d_o)
    ] + [d_gate_w, d_up_w, d_down.astype(f32)]
    return (output, input_gradient, *grads, d_gains[0], d_gains[1])


def solution(mesh):
    rows = P("dp", ("ctx", "tp"), None)
    columns, across = P(None, "tp"), P("tp", None)
    return jax.shard_map(
        on_device,
        mesh=mesh,
        in_specs=(
            rows, P("dp", None), columns, columns, columns, across, columns, columns, across, P(), P(), rows,
        ),
        out_specs=(rows, rows, columns, columns, columns, across, columns, columns, across, P(), P()),
        check_vma=False,
    )
```

```python
import functools
import math

import jax
import jax.numpy as jnp
from jax import lax
from jax.experimental import pallas as pl
from jax.experimental.pallas import tpu as pltpu
from jax.sharding import PartitionSpec as P

HEAD = 64
LANES = 128
epsilon = 1e-05
negative = -1e30
plain = (((1,), (0,)), ((), ()))
contract_first = (((0,), (0,)), ((), ()))
contract_last = (((1,), (1,)), ((), ()))
bf16 = jnp.bfloat16
f32 = jnp.float32
barrier = lax.optimization_barrier
CHUNKS = 2


def dot(left, right, dims=plain):
    return lax.dot_general(left, right, dims, preferred_element_type=f32)


def rope_tables(positions):
    half = HEAD // 2
    steps = jnp.arange(half, dtype=f32)
    base = jnp.power(f32(500000.0), -2.0 * steps / HEAD)
    wavelen = 2.0 * math.pi / base
    smooth = (8192.0 / wavelen - 1.0) / 3.0
    between = (1.0 - smooth) * base / 32.0 + smooth * base
    used = jnp.where(wavelen > 8192.0, base / 32.0, jnp.where(wavelen < 2048.0, base, between))
    angle = positions.astype(f32)[:, None] * jnp.tile(used, LANES // half)[None, :]
    sign = jnp.where(jnp.arange(LANES) % HEAD < half, -1.0, 1.0).astype(f32)
    return jnp.cos(angle), jnp.sin(angle) * sign[None, :]


def doc_starts(lengths_row, index):
    count = lengths_row.shape[0]
    docs = jnp.arange(count, dtype=jnp.int32)
    ends = jnp.sum(jnp.where(docs[None, :] <= docs[:, None], lengths_row[None, :], 0), 1)
    return jnp.max(jnp.where(index[:, None] >= ends[None, :], ends[None, :], 0), 1)


def swap_halves(v):
    lane = lax.broadcasted_iota(jnp.int32, v.shape, 1)
    return jnp.where(lane % HEAD < HEAD // 2, pltpu.roll(v, LANES - HEAD // 2, 1), pltpu.roll(v, HEAD // 2, 1))


def rope_kernel(q_cols, turned, x_ref, cos_ref, sin_ref, out_ref):
    cosine, sine = cos_ref[...], sin_ref[...]
    lane = lax.broadcasted_iota(jnp.int32, cosine.shape, 1)
    for at in range(0, x_ref.shape[1], LANES):
        v = x_ref[:, at : at + LANES].astype(f32)
        if at < turned:
            r = v * cosine + swap_halves(v) * sine
            v = r if at + LANES <= turned else jnp.where(lane < turned - at, r, v)
            if at < q_cols:
                v = v * HEAD**-0.5
        out_ref[:, at : at + LANES] = v.astype(bf16)


def rope(x, cosine, sine, q_cols, turned):
    rows, cols = x.shape
    step = min(rows, 256)
    return pl.pallas_call(
        functools.partial(rope_kernel, q_cols, turned),
        grid=(rows // step,),
        in_specs=[
            pl.BlockSpec((step, cols), lambda i: (i, 0)),
            pl.BlockSpec((step, LANES), lambda i: (i, 0)),
            pl.BlockSpec((step, LANES), lambda i: (i, 0)),
        ],
        out_specs=pl.BlockSpec((step, cols), lambda i: (i, 0)),
        out_shape=jax.ShapeDtypeStruct((rows, cols), bf16),
        name="rotate",
    )(x, cosine, sine)


def project_kernel(q_cols, turned, n, here, w_ref, cos_ref, sin_ref, *rest):
    pieces, (out_ref, sums) = rest[:n], rest[n:]
    shift = lax.rem(here[0] + n - pl.program_id(0), n)
    for d, piece in enumerate(pieces):

        @pl.when(shift == d)
        def _():
            sums[...] = dot(piece[...], w_ref[...])

    rope_kernel(q_cols, turned, sums, cos_ref, sin_ref, out_ref)


def project(here, pieces, w, cosine, sine, q_cols, turned):
    n, (rows, depth) = len(pieces), pieces[0].shape
    cols = w.shape[1]
    table = pl.BlockSpec((rows, LANES), lambda i, h: (i, 0))
    return pl.pallas_call(
        functools.partial(project_kernel, q_cols, turned, n),
        grid_spec=pltpu.PrefetchScalarGridSpec(
            num_scalar_prefetch=1, grid=(n,),
            in_specs=[pl.BlockSpec((depth, cols), lambda i, h: (0, 0)), table, table]
            + [pl.BlockSpec((rows, depth), lambda i, h: (0, 0))] * n,
            out_specs=pl.BlockSpec((rows, cols), lambda i, h: (i, 0)),
            scratch_shapes=[pltpu.VMEM((rows, cols), f32)],
        ),
        out_shape=jax.ShapeDtypeStruct((n * rows, cols), bf16),
        compiler_params=pltpu.CompilerParams(vmem_limit_bytes=40 * 2**20),
        cost_estimate=pl.CostEstimate(flops=2 * n * rows * depth * cols, bytes_accessed=2 * rows * depth, transcendentals=0),
        name="project",
    )(here, w, cosine, sine, *pieces)


def spread_kernel(kv, n, here, *refs):
    pieces, (both_ref, turned_ref) = refs[:n], refs[n:]
    for mask, piece in enumerate(pieces):
        rows = piece.shape[0]
        place = pl.ds(pl.multiple_of((here[0] ^ mask) * rows, rows), rows)
        for at in range(0, piece.shape[1], LANES):
            x = piece[:, at : at + LANES].astype(f32)
            other = pltpu.roll(x, HEAD, 1)
            left = lax.broadcasted_iota(jnp.int32, x.shape, 1) < HEAD
            head = at // HEAD
            both_ref[head, place, :] = jnp.where(left, x, other).astype(bf16)
            both_ref[head + 1, place, :] = jnp.where(left, other, x).astype(bf16)
            turned_ref[at : at + LANES, place] = x.T.astype(bf16)


def spread(here, pieces, kv):
    n, (rows, cols) = len(pieces), pieces[0].shape
    return pl.pallas_call(
        functools.partial(spread_kernel, kv, n),
        grid_spec=pltpu.PrefetchScalarGridSpec(
            num_scalar_prefetch=1, grid=(1,),
            in_specs=[pl.BlockSpec((rows, cols), lambda i, h: (0, 0))] * n,
            out_specs=[
                pl.BlockSpec((2 * kv, n * rows, LANES), lambda i, h: (0, 0, 0)),
                pl.BlockSpec((cols, n * rows), lambda i, h: (0, 0)),
            ],
        ),
        out_shape=[
            jax.ShapeDtypeStruct((2 * kv, n * rows, LANES), bf16),
            jax.ShapeDtypeStruct((cols, n * rows), bf16),
        ],
        compiler_params=pltpu.CompilerParams(vmem_limit_bytes=60 * 2**20),
        name="spread",
    )(here, *pieces)


def over_blocks(bounds, block, step, carry):
    b0, b1, b2, b3 = [bounds[1 + k, block] for k in range(4)]
    carry = lax.fori_loop(b0, b1, functools.partial(step, True), carry)
    carry = lax.fori_loop(b1, b2, functools.partial(step, False), carry)
    return lax.fori_loop(b2, b3, functools.partial(step, True), carry)


def allowed_keys(at, first_row, low, bk, bq):
    key = at + lax.broadcasted_iota(jnp.int32, (bk, bq), 0)
    row = first_row + lax.broadcasted_iota(jnp.int32, (bk, bq), 1)
    return (key <= row) & (key >= low)


def halves(x):
    left = lax.broadcasted_iota(jnp.int32, x.shape, 1) < HEAD
    zero = jnp.zeros_like(x)
    return [jnp.where(left, x, zero), jnp.where(left, zero, x)]


def attend_kernel(bq, bk, bounds, q_ref, low_ref, k_ref, vt_ref, o_ref, lse_ref):
    block = pl.program_id(0)
    pairs = q_ref.shape[1] // LANES
    heads = range(2 * pairs)
    q = sum([halves(q_ref[:, p * LANES : (p + 1) * LANES]) for p in range(pairs)], [])

    def step(masked, j, carry):
        peaks, totals, accs = carry
        at = pl.multiple_of(j * bk, bk)
        if masked:
            ok = allowed_keys(at, bounds[0, block], low_ref[:1, :], bk, bq)
        k = k_ref[0, pl.ds(at, bk), :]
        scores = [dot(k, q[h], contract_last) for h in heads]
        new_peaks, new_totals, new_accs = [], [], []
        for h in heads:
            s = scores[h]
            if masked:
                s = jnp.where(ok, s, negative)
            peak = jnp.maximum(peaks[h], jnp.max(s, 0, keepdims=True))
            p = jnp.exp(s - peak)
            if masked:
                p = jnp.where(ok, p, 0.0)
            decay = jnp.exp(peaks[h] - peak)
            new_peaks.append(peak)
            new_totals.append(totals[h] * decay + jnp.sum(p, 0, keepdims=True))
            new_accs.append(accs[h] * decay + dot(vt_ref[:, pl.ds(at, bk)], p.astype(bf16)))
        return tuple(new_peaks), tuple(new_totals), tuple(new_accs)

    start = [(jnp.full((1, bq), negative, f32),) * len(heads), (jnp.zeros((1, bq), f32),) * len(heads)]
    start.append((jnp.zeros((HEAD, bq), f32),) * len(heads))
    peaks, totals, accs = over_blocks(bounds, block, step, tuple(start))
    for p in range(pairs):
        pair = [accs[h] / totals[h] for h in (2 * p, 2 * p + 1)]
        o_ref[:, p * LANES : (p + 1) * LANES] = jnp.concatenate(pair, 0).T.astype(bf16)
    for h in heads:
        lse_ref[h // 2, h % 2 : h % 2 + 1, :] = peaks[h] + jnp.log(totals[h])


def attend(bounds, queries, low, both, turned, g, kv, bq, bk):
    rows, keys = queries.shape[0], both.shape[1]
    cols = queries.shape[1] // kv
    pairs = cols // LANES
    size = rows * cols * keys
    return pl.pallas_call(
        functools.partial(attend_kernel, bq, bk),
        grid_spec=pltpu.PrefetchScalarGridSpec(
            num_scalar_prefetch=1, grid=(rows // bq,),
            in_specs=[
                pl.BlockSpec((bq, cols), lambda i, b: (i, g)),
                pl.BlockSpec((8, bq), lambda i, b: (0, i)),
                pl.BlockSpec((1, keys, LANES), lambda i, b: (g, 0, 0)),
                pl.BlockSpec((HEAD, keys), lambda i, b: (kv + g, 0)),
            ],
            out_specs=[
                pl.BlockSpec((bq, cols), lambda i, b: (i, 0)),
                pl.BlockSpec((pairs, 8, bq), lambda i, b: (0, 0, i)),
            ],
        ),
        out_shape=[
            jax.ShapeDtypeStruct((rows, cols), bf16),
            jax.ShapeDtypeStruct((pairs, 8, rows), f32),
        ],
        compiler_params=pltpu.CompilerParams(vmem_limit_bytes=60 * 2**20),
        cost_estimate=pl.CostEstimate(flops=4 * size, bytes_accessed=8 * rows * cols, transcendentals=size // HEAD),
        name="attend",
    )(bounds, queries, low, both, turned)


def attend_back_kernel(
    bq, bk, pieces, bounds, q_ref, o_ref, low_ref, lse_ref, cos_ref, sin_ref, k_ref, kt_ref, v_ref, *rest
):
    do_refs, (dq_ref, dk_ref, dv_ref, do_rows) = rest[:pieces], rest[pieces:]
    pair, block = pl.program_id(0), pl.program_id(1)

    @pl.when((pair == 0) & (block == 0))
    def _():
        dk_ref[...] = jnp.zeros_like(dk_ref)
        dv_ref[...] = jnp.zeros_like(dv_ref)

    @pl.when(block == 0)
    def _():
        for shift, do_ref in enumerate(do_refs):
            rows = do_ref.shape[0]
            place = lax.rem(bounds[5, 0] + pieces - shift, pieces) * rows
            do_rows[pl.ds(pl.multiple_of(place, rows), rows), :] = do_ref[...]

    do = do_rows[pl.ds(pl.multiple_of(block * bq, bq), bq), :]
    q_of, do_of = halves(q_ref[...]), halves(do)
    product = do.astype(f32) * o_ref[...].astype(f32)
    high = product.astype(bf16)
    low = (product - high.astype(f32)).astype(bf16)
    row = lax.broadcasted_iota(jnp.int32, (8, LANES), 0)
    lane = lax.broadcasted_iota(jnp.int32, (8, LANES), 1)
    ones = jnp.where(lane // HEAD == row, 1.0, 0.0).astype(bf16)
    delta = dot(ones, high, contract_last) + dot(ones, low, contract_last)

    def step(masked, j, accs):
        at = pl.multiple_of(j * bk, bk)
        here = pl.ds(at, bk)
        if masked:
            ok = allowed_keys(at, bounds[0, block], low_ref[:1, :], bk, bq)
        k, v = k_ref[0, here, :], v_ref[0, here, :]
        scores = [dot(k, q_of[h], contract_last) for h in range(2)]
        d_probs = [dot(v, do_of[h], contract_last) for h in range(2)]
        dk, dv, new = [], [], []
        for h in range(2):
            p = jnp.exp(scores[h] - lse_ref[0, h : h + 1, :])
            if masked:
                p = jnp.where(ok, p, 0.0)
            ds = (p * (d_probs[h] - delta[h : h + 1, :])).astype(bf16)
            dv.append(dot(p.astype(bf16), do_of[h]))
            dk.append(dot(ds, q_of[h]))
            new.append(accs[h] + dot(kt_ref[:, here], ds))
        dk_ref[here, :] += dk[0] + dk[1]
        dv_ref[here, :] += dv[0] + dv[1]
        return tuple(new)

    accs = over_blocks(bounds, block, step, (jnp.zeros((HEAD, bq), f32),) * 2)
    g = jnp.concatenate(accs, 0).T
    dq_ref[...] = ((g * cos_ref[...] - swap_halves(g) * sin_ref[...]) * HEAD**-0.5).astype(bf16)


def attend_back(bounds, queries, attended, low, sums, cosine, sine, both, turned, d_attended, g, kv, bq, bk):
    rows, keys = queries.shape[0], both.shape[1]
    cols = queries.shape[1] // kv
    pairs, pieces = cols // LANES, len(d_attended)
    mine = pl.BlockSpec((bq, LANES), lambda p, i, b: (i, p))
    table = pl.BlockSpec((bq, LANES), lambda p, i, b: (i, 0))
    head = lambda at: pl.BlockSpec((1, keys, LANES), lambda p, i, b: (at, 0, 0))
    whole = pl.BlockSpec((keys, LANES), lambda p, i, b: (0, 0))
    size = rows * cols * keys
    return pl.pallas_call(
        functools.partial(attend_back_kernel, bq, bk, pieces),
        grid_spec=pltpu.PrefetchScalarGridSpec(
            num_scalar_prefetch=1, grid=(pairs, rows // bq),
            in_specs=[
                pl.BlockSpec((bq, LANES), lambda p, i, b: (i, g * pairs + p)), mine,
                pl.BlockSpec((8, bq), lambda p, i, b: (0, i)), pl.BlockSpec((1, 8, bq), lambda p, i, b: (p, 0, i)),
                table, table, head(g), pl.BlockSpec((HEAD, keys), lambda p, i, b: (g, 0)), head(kv + g),
            ] + [pl.BlockSpec((rows // pieces, LANES), lambda p, i, b: (0, g * pairs + p))] * pieces,
            out_specs=[mine, whole, whole],
            scratch_shapes=[pltpu.VMEM((rows, LANES), bf16)],
        ),
        out_shape=[jax.ShapeDtypeStruct((rows, cols), bf16)] + [jax.ShapeDtypeStruct((keys, LANES), f32)] * 2,
        compiler_params=pltpu.CompilerParams(vmem_limit_bytes=60 * 2**20),
        cost_estimate=pl.CostEstimate(flops=size, bytes_accessed=8 * rows * cols, transcendentals=size // HEAD),
        name="attend_back",
    )(bounds, queries, attended, low, sums, cosine, sine, both, turned, both, *d_attended)


def block_bounds(starts, low, bq, bk, tp_me):
    low = low.reshape(-1, bq)
    begin, end = low[:, 0] // bk, (starts + bq + bk - 1) // bk
    whole = jnp.clip((low[:, -1] + bk - 1) // bk, begin, end)
    diagonal = jnp.clip((starts + 1) // bk, whole, end)
    return jnp.stack([starts, begin, whole, diagonal, end, jnp.full_like(starts, tp_me)]).astype(jnp.int32)


def ffn_kernel(tiles, earlier, x_ref, c_ref, gate_ref, up_ref, down_ref, *rest):
    act_ref, d_gate_ref, d_up_ref, out_ref, acc = rest[earlier:]
    tile = pl.program_id(0)
    x = x_ref[...]
    c = c_ref[...].reshape(x.shape)
    gate, up = dot(x, gate_ref[...]), dot(x, up_ref[...])
    d_act = dot(c, down_ref[...], contract_last)
    sig = 1.0 / (1.0 + jnp.exp(-gate))
    swish = gate * sig
    d_gate = (d_act * up * sig * (1.0 + gate * (1.0 - sig))).astype(bf16)
    d_up = (d_act * swish).astype(bf16)
    act_ref[...] = (swish * up).astype(bf16).reshape(act_ref.shape)
    d_gate_ref[...] = d_gate.reshape(act_ref.shape)
    d_up_ref[...] = d_up.reshape(act_ref.shape)
    part = dot(d_gate, gate_ref[...], contract_last) + dot(d_up, up_ref[...], contract_last)

    @pl.when(tile == 0)
    def _():
        acc[...] = part

    @pl.when(tile > 0)
    def _():
        acc[...] += part

    @pl.when(tile == tiles - 1)
    def _():
        out_ref[...] = acc[...].astype(bf16)


def ffn_chunk(x, c, gate_weight, up_weight, down_weight, chunk, earlier):
    rows, width = x.shape
    groups, own = c.shape[:2]
    hidden = gate_weight.shape[1]
    tn = min(512, hidden)
    tiles, part = hidden // tn, rows // groups
    column = pl.BlockSpec((width, tn), lambda j: (0, j))
    result = pl.BlockSpec((groups, part, tn), lambda j: (0, chunk, j))
    whole = pl.BlockSpec((rows, width), lambda j: (0, 0))
    return pl.pallas_call(
        functools.partial(ffn_kernel, tiles, len(earlier)),
        grid=(tiles,),
        in_specs=[
            whole, pl.BlockSpec((groups, part, width), lambda j: (0, chunk, 0)), column, column,
            pl.BlockSpec((tn, width), lambda j: (j, 0)),
        ] + [pl.BlockSpec(memory_space=pl.ANY)] * len(earlier),
        out_specs=[result] * 3 + [whole],
        scratch_shapes=[pltpu.VMEM((rows, width), f32)],
        out_shape=[jax.ShapeDtypeStruct((groups, own, hidden), bf16)] * 3
        + [jax.ShapeDtypeStruct((rows, width), bf16)],
        input_output_aliases={5 + i: i for i in range(len(earlier))},
        compiler_params=pltpu.CompilerParams(vmem_limit_bytes=60 * 2**20),
        cost_estimate=pl.CostEstimate(
            flops=16 * rows * width * hidden, bytes_accessed=6 * width * hidden, transcendentals=rows * hidden
        ),
        name="feed_forward",
    )(x, c, gate_weight, up_weight, down_weight, *earlier)


def branch_kernel(shifts, attended_ref, o_ref, x_ref, gain_ref, mid_ref, unit_ref, normed_ref, rstd_ref):
    shift = pl.program_id(0)
    o = o_ref[...].reshape(-1, mid_ref.shape[1])
    groups, wide = attended_ref.shape[1], attended_ref.shape[3]
    part = sum(dot(attended_ref[0, g], o[g * wide : (g + 1) * wide]) for g in range(groups))

    @pl.when(shift == 0)
    def _():
        mid_ref[...] = x_ref[...].astype(f32) + part

    @pl.when(shift > 0)
    def _():
        mid_ref[...] += part

    @pl.when(shift == shifts - 1)
    def _():
        mid = mid_ref[...]
        rstd = lax.rsqrt(jnp.mean(mid * mid, -1, keepdims=True) + epsilon)
        unit = mid * rstd
        unit_ref[...] = unit
        normed_ref[...] = (unit * gain_ref[...]).astype(bf16)
        rstd_ref[...] = jnp.broadcast_to(rstd, rstd_ref.shape)


def branch(attended, o, x, gain):
    shifts, groups, own, wide = attended.shape
    plane, _, rows, width = o.shape
    whole = lambda cols: pl.BlockSpec((own, cols), lambda d: (0, 0))
    shapes = [((own, width), f32), ((own, width), f32), ((own, width), bf16), ((own, LANES), f32)]
    return pl.pallas_call(
        functools.partial(branch_kernel, shifts),
        grid=(shifts,),
        in_specs=[
            pl.BlockSpec((1, groups, own, wide), lambda d: (d, 0, 0, 0)),
            pl.BlockSpec((plane, 1, rows, width), lambda d: (0, d, 0, 0)),
            whole(width), pl.BlockSpec((1, width), lambda d: (0, 0)),
        ],
        out_specs=[whole(shape[1]) for shape, _ in shapes],
        out_shape=[jax.ShapeDtypeStruct(*shape) for shape in shapes],
        compiler_params=pltpu.CompilerParams(vmem_limit_bytes=60 * 2**20),
        name="branch",
    )(attended, o, x, gain[None])


def branch_back_kernel(x_ref, o_ref, out_ref):
    out_ref[0] = dot(x_ref[...], o_ref[...].reshape(-1, x_ref.shape[1]), contract_last).astype(bf16)


def branch_back(x, o):
    plane, shifts, rows, width = o.shape
    own = x.shape[0]
    return pl.pallas_call(
        branch_back_kernel,
        grid=(shifts,),
        in_specs=[
            pl.BlockSpec((own, width), lambda d: (0, 0)),
            pl.BlockSpec((plane, 1, rows, width), lambda d: (0, lax.rem(shifts - d, shifts), 0, 0)),
        ],
        out_specs=pl.BlockSpec((1, own, plane * rows), lambda d: (d, 0, 0)),
        out_shape=jax.ShapeDtypeStruct((shifts, own, plane * rows), bf16),
        compiler_params=pltpu.CompilerParams(vmem_limit_bytes=60 * 2**20),
        name="branch_back",
    )(x, o)


def bits_of(n):
    return [1 << b for b in range(n.bit_length() - 1)]


def exchange(x, axis, bit):
    n = lax.axis_size(axis)
    return lax.ppermute(x, axis, [(i, i ^ bit) for i in range(n)])


def gather_ctx(x):
    n = lax.axis_size("ctx")
    held = {0: x}
    for bit in reversed(bits_of(n)):
        held.update({mask ^ bit: exchange(piece, "ctx", bit) for mask, piece in held.items()})
    return [held[mask] for mask in range(n)]


def scatter_sum_ctx(x):
    n, me = lax.axis_size("ctx"), lax.axis_index("ctx")
    x = x.reshape(n, -1, x.shape[1])
    for bit in bits_of(n):
        x = x.reshape(-1, 2, *x.shape[1:])
        mine = (me // bit) % 2
        send = lax.dynamic_index_in_dim(x, 1 - mine, 1, False)
        keep = lax.dynamic_index_in_dim(x, mine, 1, False)
        x = (keep.astype(f32) + exchange(send, "ctx", bit).astype(f32)).astype(bf16)
    return x[0]


def mirror_ctx(x):
    n = lax.axis_size("ctx")
    return lax.ppermute(x, "ctx", [(i, n - 1 - i) for i in range(n)])


def home_pairs(n_ctx, n_tp, shift):
    pairs = []
    for c in range(n_ctx):
        for t in range(n_tp):
            to = (t + shift) % n_tp
            pairs.append((c * n_tp + t, (c if to < n_tp // 2 else n_ctx - 1 - c) * n_tp + to))
    return pairs


def to_tokens(x):
    n, me = lax.axis_size("tp"), lax.axis_index("tp")
    x = x.reshape(n, -1, x.shape[1])
    out = []
    for d in range(n):
        piece = lax.dynamic_index_in_dim(x, (me + d) % n, 0, False)
        out.append(lax.ppermute(piece, ("ctx", "tp"), home_pairs(lax.axis_size("ctx"), n, d)))
    return out


def to_heads(pieces):
    n, n_ctx = lax.axis_size("tp"), lax.axis_size("ctx")
    out = []
    for d, piece in enumerate(pieces):
        pairs = [(to, at) for at, to in home_pairs(n_ctx, n, (n - d) % n)]
        out.append(lax.ppermute(piece, ("ctx", "tp"), pairs))
    return out


def shift_tp(x, d):
    n = lax.axis_size("tp")
    return lax.ppermute(x, "tp", [(i, (i + d) % n) for i in range(n)]) if d else x


def ring_tp(x):
    n, me = lax.axis_size("tp"), lax.axis_index("tp")
    up, down = [x], [x]
    for step in range(1, n):
        up.append(lax.ppermute(up[-1], "tp", [(i, i + 1) for i in range(step - 1, n - 1)]))
        down.append(lax.ppermute(down[-1], "tp", [(i, i - 1) for i in range(1, n - step + 1)]))
    return [x] + [jnp.where(me >= d, up[d], down[n - d]) for d in range(1, n)]


def in_order(pieces):
    n, me = lax.axis_size("tp"), lax.axis_index("tp")
    pieces = jnp.stack(pieces)
    return jnp.concatenate([lax.dynamic_index_in_dim(pieces, (me - t) % n, 0, False) for t in range(n)], 0)


def scatter_direct(x):
    n, me = lax.axis_size("tp"), lax.axis_index("tp")
    x = x.reshape(n, -1, x.shape[1])
    return sum(shift_tp(lax.dynamic_index_in_dim(x, (me + d) % n, 0, False), d).astype(f32) for d in range(n))


def gather_direct(x):
    return in_order([shift_tp(x, d) for d in range(lax.axis_size("tp"))])


def share_rows(weight):
    n, plane = lax.axis_size("tp"), lax.axis_size("dp") * lax.axis_size("ctx")
    at = lax.axis_index("dp") * lax.axis_size("ctx") + lax.axis_index("ctx")
    share = lax.dynamic_index_in_dim(weight.reshape(plane, -1, weight.shape[1]), at, 0, False)
    return jnp.concatenate([shift_tp(share, d) for d in range(n)], 0)


def gather_shares(shares):
    n = lax.axis_size("tp")
    whole = lax.all_gather(shares, ("dp", "ctx"), axis=0, tiled=True)
    return whole.reshape(-1, n, shares.shape[0] // n, shares.shape[1])


PLANE = ("dp", "ctx")


def sum_plane(*xs):
    return lax.psum(xs, PLANE)


def sum_all(x):
    for axis in ("ctx", "tp", "dp"):
        for bit in bits_of(lax.axis_size(axis)):
            x = x + exchange(x, axis, bit)
    return x


def norm_back(grad, unit, inverse_root, gain):
    scaled = grad * gain
    return inverse_root * (scaled - unit * jnp.mean(scaled * unit, -1, keepdims=True))


def gather_tp(x):
    return lax.all_gather(x, "tp", axis=0, tiled=True)


def scatter_tp(x):
    return lax.psum_scatter(x, "tp", scatter_dimension=0, tiled=True)


def on_device(
    tokens, lengths, q_weight, k_weight, v_weight, o_weight, gate_weight, up_weight, down_weight,
    attention_gain, ffn_gain, cotangent,
):
    ctx, me = lax.axis_size("ctx"), lax.axis_index("ctx")
    own = tokens.shape[1]
    block = own * lax.axis_size("tp")
    half = block // 2
    q_cols, kv_cols = q_weight.shape[1], k_weight.shape[1]
    kv = kv_cols // HEAD

    x = tokens[0].astype(f32)
    rstd1 = lax.rsqrt(jnp.mean(x * x, -1, keepdims=True) + epsilon)
    unit1 = x * rstd1
    pieces = ring_tp((unit1 * attention_gain).astype(bf16))
    o_full = gather_shares(share_rows(o_weight))
    w_kv = jnp.concatenate([k_weight, v_weight], 1)

    index = me * block + jnp.arange(block, dtype=jnp.int32)
    cosine, sine = rope_tables(index - doc_starts(lengths[0], index))
    far = (2 * ctx - 1 - 2 * me) * half
    near = me * block
    steps = jnp.arange(half, dtype=jnp.int32)
    q_index = jnp.concatenate([near + steps, far + steps])
    q_low = doc_starts(lengths[0], q_index)
    q_cos, q_sin = rope_tables(q_index - q_low)
    bq = bk = min(512, half)
    bounds = block_bounds(q_index.reshape(-1, bq)[:, 0], q_low, bq, bk, lax.axis_index("tp"))
    low_rows = jnp.broadcast_to(q_low[None, :], (8, block))
    pieces, w_kv, cosine, sine, q_cos, q_sin, bounds, low_rows = barrier(
        (pieces, w_kv, cosine, sine, q_cos, q_sin, bounds, low_rows)
    )
    here = lax.axis_index("tp")[None]
    kv_own = project(here, pieces, w_kv, cosine, sine, 0, kv_cols)
    kv_all = gather_ctx(kv_own)
    pieces, o_full = barrier((pieces, o_full))
    q_own = project(here, pieces, q_weight, cosine, sine, q_cols, q_cols)
    normed = in_order(pieces)
    queries = jnp.concatenate([q_own[:half], mirror_ctx(q_own[half:])], 0)
    c_own, _ = barrier((cotangent[0], o_full))
    c_full = gather_tp(c_own)
    both, turned = spread(me[None], kv_all, kv)
    parts = [attend(bounds, queries, low_rows, both, turned, g, kv, bq, bk) for g in range(kv)]
    sent = [to_tokens(attended) for attended, _ in parts]
    attended_own = jnp.stack([jnp.stack(pieces) for pieces in zip(*sent)])
    attended_own, c_full = barrier((attended_own, c_full))
    attended_z = jnp.concatenate([attended for attended, _ in parts], 1)
    attended = jnp.concatenate([attended_z[:half], mirror_ctx(attended_z[half:])], 0)

    mid, unit2, ffn_own, rstd2 = branch(attended_own, o_full, tokens[0], ffn_gain)
    rstd2 = rstd2[:, :1]
    part = own // CHUNKS
    tp = lax.axis_size("tp")
    c_rows = c_full.reshape(tp, own, -1)
    gathered, hidden, scattered = [], [], []
    for chunk in range(CHUNKS):
        piece = ffn_own[chunk * part : (chunk + 1) * part]
        if gathered:
            piece, _ = barrier((piece, gathered[-1]))
        gathered.append(gather_tp(piece))
    for chunk in range(CHUNKS):
        *hidden, out = ffn_chunk(gathered[chunk], c_rows, gate_weight, up_weight, down_weight, chunk, hidden)
        scattered.append(scatter_direct(out) if chunk == CHUNKS - 1 else scatter_tp(out).astype(f32))
    act, d_gate, d_up = [h.reshape(block, -1) for h in hidden]
    d_ffn = jnp.concatenate(scattered, 0)
    ffn_normed = jnp.stack([g.reshape(tp, part, -1) for g in gathered], 1).reshape(block, -1)

    d_mid = c_own.astype(f32) + norm_back(d_ffn, unit2, rstd2, ffn_gain)
    ffn_gain_part = jnp.sum(d_ffn * unit2, 0)
    d_gate_w = dot(ffn_normed, d_gate, contract_first).astype(bf16)
    d_up_w = dot(ffn_normed, d_up, contract_first).astype(bf16)
    d_branch, _ = barrier((d_mid.astype(bf16), (d_gate_w, d_up_w)))
    d_gate_w, d_up_w = sum_plane(d_gate_w, d_up_w)
    d_attended = to_heads(list(branch_back(d_branch, o_full)))
    d_branch, d_attended = barrier((d_branch, d_attended))
    d_branch = gather_direct(d_branch)
    d_down = dot(act, c_full, contract_first).astype(bf16)

    act_late, _ = barrier((act, d_branch))
    out_sum = scatter_direct(dot(act_late, down_weight).astype(bf16))

    d_o = dot(attended, d_branch, contract_first).astype(bf16)
    back = [
        attend_back(
            bounds, queries, parts[g][0], low_rows, parts[g][1], q_cos, q_sin, both, turned, d_attended, g, kv, bq, bk
        )
        for g in range(kv)
    ]
    d_q = jnp.concatenate([dq for dq, _, _ in back], 1)
    d_q = jnp.concatenate([d_q[:half], mirror_ctx(d_q[half:])], 0)
    d_kv = jnp.concatenate([back[g][i][:, :HEAD] + back[g][i][:, HEAD:] for i in (1, 2) for g in range(kv)], 1)
    d_kv = rope(scatter_sum_ctx(d_kv.astype(bf16)), cosine, -sine, 0, kv_cols)
    d_normed_part = dot(d_q, q_weight, contract_last) + dot(d_kv, w_kv, contract_last)
    d_normed_part, out_sum = barrier((d_normed_part.astype(bf16), out_sum))
    d_normed = scatter_direct(d_normed_part)
    d_qkv_w = dot(normed, jnp.concatenate([d_q, d_kv], 1), contract_first).astype(bf16)
    d_qkv_w, d_o, d_down, _ = barrier((d_qkv_w, d_o, d_down, (d_gate_w, d_up_w)))
    d_gate_w, d_up_w = d_gate_w.astype(f32), d_up_w.astype(f32)
    d_qkv_w, d_o, d_down = sum_plane(d_qkv_w, d_o, d_down)

    out_sum, _ = barrier((out_sum, (d_gate_w, d_up_w)))
    output = (mid + out_sum).astype(bf16)[None]
    d_normed, _ = barrier((d_normed, output))
    input_gradient = (d_mid + norm_back(d_normed, unit1, rstd1, attention_gain)).astype(bf16)[None]
    attn_gain_part = jnp.sum(d_normed * unit1, 0)
    d_gains = sum_all(jnp.stack([attn_gain_part, ffn_gain_part]))
    d_q_w, d_kv_w = d_qkv_w[:, :q_cols], d_qkv_w[:, q_cols:]
    grads = [
        g.astype(f32)
        for g in (d_q_w, d_kv_w[:, :kv_cols], d_kv_w[:, kv_cols:], d_o)
    ] + [d_gate_w, d_up_w, d_down.astype(f32)]
    return (output, input_gradient, *grads, d_gains[0], d_gains[1])


def solution(mesh):
    rows = P("dp", ("ctx", "tp"), None)
    columns, across = P(None, "tp"), P("tp", None)
    return jax.shard_map(
        on_device,
        mesh=mesh,
        in_specs=(
            rows, P("dp", None), columns, columns, columns, across, columns, columns, across, P(), P(), rows,
        ),
        out_specs=(rows, rows, columns, columns, columns, across, columns, columns, across, P(), P()),
        check_vma=False,
    )
```

```python
import functools
import math

import jax
import jax.numpy as jnp
from jax import lax
from jax.experimental import pallas as pl
from jax.experimental.pallas import tpu as pltpu
from jax.sharding import PartitionSpec as P

HEAD = 64
LANES = 128
epsilon = 1e-05
negative = -1e30
plain = (((1,), (0,)), ((), ()))
contract_first = (((0,), (0,)), ((), ()))
contract_last = (((1,), (1,)), ((), ()))
bf16 = jnp.bfloat16
f32 = jnp.float32
barrier = lax.optimization_barrier
CHUNKS = 2


def dot(left, right, dims=plain):
    return lax.dot_general(left, right, dims, preferred_element_type=f32)


def rope_tables(positions):
    half = HEAD // 2
    steps = jnp.arange(half, dtype=f32)
    base = jnp.power(f32(500000.0), -2.0 * steps / HEAD)
    wavelen = 2.0 * math.pi / base
    smooth = (8192.0 / wavelen - 1.0) / 3.0
    between = (1.0 - smooth) * base / 32.0 + smooth * base
    used = jnp.where(wavelen > 8192.0, base / 32.0, jnp.where(wavelen < 2048.0, base, between))
    angle = positions.astype(f32)[:, None] * jnp.tile(used, LANES // half)[None, :]
    sign = jnp.where(jnp.arange(LANES) % HEAD < half, -1.0, 1.0).astype(f32)
    return jnp.cos(angle), jnp.sin(angle) * sign[None, :]


def doc_starts(lengths_row, index):
    count = lengths_row.shape[0]
    docs = jnp.arange(count, dtype=jnp.int32)
    ends = jnp.sum(jnp.where(docs[None, :] <= docs[:, None], lengths_row[None, :], 0), 1)
    return jnp.max(jnp.where(index[:, None] >= ends[None, :], ends[None, :], 0), 1)


def swap_halves(v):
    lane = lax.broadcasted_iota(jnp.int32, v.shape, 1)
    return jnp.where(lane % HEAD < HEAD // 2, pltpu.roll(v, LANES - HEAD // 2, 1), pltpu.roll(v, HEAD // 2, 1))


def rope_kernel(q_cols, turned, x_ref, cos_ref, sin_ref, out_ref):
    cosine, sine = cos_ref[...], sin_ref[...]
    lane = lax.broadcasted_iota(jnp.int32, cosine.shape, 1)
    for at in range(0, x_ref.shape[1], LANES):
        v = x_ref[:, at : at + LANES].astype(f32)
        if at < turned:
            r = v * cosine + swap_halves(v) * sine
            v = r if at + LANES <= turned else jnp.where(lane < turned - at, r, v)
            if at < q_cols:
                v = v * HEAD**-0.5
        out_ref[:, at : at + LANES] = v.astype(bf16)


def rope(x, cosine, sine, q_cols, turned):
    rows, cols = x.shape
    step = min(rows, 256)
    return pl.pallas_call(
        functools.partial(rope_kernel, q_cols, turned),
        grid=(rows // step,),
        in_specs=[
            pl.BlockSpec((step, cols), lambda i: (i, 0)),
            pl.BlockSpec((step, LANES), lambda i: (i, 0)),
            pl.BlockSpec((step, LANES), lambda i: (i, 0)),
        ],
        out_specs=pl.BlockSpec((step, cols), lambda i: (i, 0)),
        out_shape=jax.ShapeDtypeStruct((rows, cols), bf16),
        name="rotate",
    )(x, cosine, sine)


def project_kernel(q_cols, turned, n, here, w_ref, cos_ref, sin_ref, *rest):
    pieces, (out_ref, sums) = rest[:n], rest[n:]
    shift = lax.rem(here[0] + n - pl.program_id(0), n)
    for d, piece in enumerate(pieces):

        @pl.when(shift == d)
        def _():
            sums[...] = dot(piece[...], w_ref[...])

    rope_kernel(q_cols, turned, sums, cos_ref, sin_ref, out_ref)


def project(here, pieces, w, cosine, sine, q_cols, turned):
    n, (rows, depth) = len(pieces), pieces[0].shape
    cols = w.shape[1]
    table = pl.BlockSpec((rows, LANES), lambda i, h: (i, 0))
    return pl.pallas_call(
        functools.partial(project_kernel, q_cols, turned, n),
        grid_spec=pltpu.PrefetchScalarGridSpec(
            num_scalar_prefetch=1, grid=(n,),
            in_specs=[pl.BlockSpec((depth, cols), lambda i, h: (0, 0)), table, table]
            + [pl.BlockSpec((rows, depth), lambda i, h: (0, 0))] * n,
            out_specs=pl.BlockSpec((rows, cols), lambda i, h: (i, 0)),
            scratch_shapes=[pltpu.VMEM((rows, cols), f32)],
        ),
        out_shape=jax.ShapeDtypeStruct((n * rows, cols), bf16),
        compiler_params=pltpu.CompilerParams(vmem_limit_bytes=40 * 2**20),
        cost_estimate=pl.CostEstimate(flops=2 * n * rows * depth * cols, bytes_accessed=2 * rows * depth, transcendentals=0),
        name="project",
    )(here, w, cosine, sine, *pieces)


def spread_kernel(kv, n, here, *refs):
    pieces, (both_ref, turned_ref) = refs[:n], refs[n:]
    for mask, piece in enumerate(pieces):
        rows = piece.shape[0]
        place = pl.ds(pl.multiple_of((here[0] ^ mask) * rows, rows), rows)
        for at in range(0, piece.shape[1], LANES):
            x = piece[:, at : at + LANES].astype(f32)
            other = pltpu.roll(x, HEAD, 1)
            left = lax.broadcasted_iota(jnp.int32, x.shape, 1) < HEAD
            head = at // HEAD
            both_ref[head, place, :] = jnp.where(left, x, other).astype(bf16)
            both_ref[head + 1, place, :] = jnp.where(left, other, x).astype(bf16)
            turned_ref[at : at + LANES, place] = x.T.astype(bf16)


def spread(here, pieces, kv):
    n, (rows, cols) = len(pieces), pieces[0].shape
    return pl.pallas_call(
        functools.partial(spread_kernel, kv, n),
        grid_spec=pltpu.PrefetchScalarGridSpec(
            num_scalar_prefetch=1, grid=(1,),
            in_specs=[pl.BlockSpec((rows, cols), lambda i, h: (0, 0))] * n,
            out_specs=[
                pl.BlockSpec((2 * kv, n * rows, LANES), lambda i, h: (0, 0, 0)),
                pl.BlockSpec((cols, n * rows), lambda i, h: (0, 0)),
            ],
        ),
        out_shape=[
            jax.ShapeDtypeStruct((2 * kv, n * rows, LANES), bf16),
            jax.ShapeDtypeStruct((cols, n * rows), bf16),
        ],
        compiler_params=pltpu.CompilerParams(vmem_limit_bytes=60 * 2**20),
        name="spread",
    )(here, *pieces)


def over_blocks(bounds, block, step, carry):
    b0, b1, b2, b3 = [bounds[1 + k, block] for k in range(4)]
    carry = lax.fori_loop(b0, b1, functools.partial(step, True), carry)
    carry = lax.fori_loop(b1, b2, functools.partial(step, False), carry)
    return lax.fori_loop(b2, b3, functools.partial(step, True), carry)


def allowed_keys(at, first_row, low, bk, bq):
    key = at + lax.broadcasted_iota(jnp.int32, (bk, bq), 0)
    row = first_row + lax.broadcasted_iota(jnp.int32, (bk, bq), 1)
    return (key <= row) & (key >= low)


def halves(x):
    left = lax.broadcasted_iota(jnp.int32, x.shape, 1) < HEAD
    zero = jnp.zeros_like(x)
    return [jnp.where(left, x, zero), jnp.where(left, zero, x)]


def attend_kernel(bq, bk, bounds, q_ref, low_ref, k_ref, vt_ref, o_ref, lse_ref):
    block = pl.program_id(0)
    pairs = q_ref.shape[1] // LANES
    heads = range(2 * pairs)
    q = sum([halves(q_ref[:, p * LANES : (p + 1) * LANES]) for p in range(pairs)], [])

    def step(masked, j, carry):
        peaks, totals, accs = carry
        at = pl.multiple_of(j * bk, bk)
        if masked:
            ok = allowed_keys(at, bounds[0, block], low_ref[:1, :], bk, bq)
        k = k_ref[0, pl.ds(at, bk), :]
        scores = [dot(k, q[h], contract_last) for h in heads]
        new_peaks, new_totals, new_accs = [], [], []
        for h in heads:
            s = scores[h]
            if masked:
                s = jnp.where(ok, s, negative)
            peak = jnp.maximum(peaks[h], jnp.max(s, 0, keepdims=True))
            p = jnp.exp(s - peak)
            if masked:
                p = jnp.where(ok, p, 0.0)
            decay = jnp.exp(peaks[h] - peak)
            new_peaks.append(peak)
            new_totals.append(totals[h] * decay + jnp.sum(p, 0, keepdims=True))
            new_accs.append(accs[h] * decay + dot(vt_ref[:, pl.ds(at, bk)], p.astype(bf16)))
        return tuple(new_peaks), tuple(new_totals), tuple(new_accs)

    start = [(jnp.full((1, bq), negative, f32),) * len(heads), (jnp.zeros((1, bq), f32),) * len(heads)]
    start.append((jnp.zeros((HEAD, bq), f32),) * len(heads))
    peaks, totals, accs = over_blocks(bounds, block, step, tuple(start))
    for p in range(pairs):
        pair = [accs[h] / totals[h] for h in (2 * p, 2 * p + 1)]
        o_ref[:, p * LANES : (p + 1) * LANES] = jnp.concatenate(pair, 0).T.astype(bf16)
    for h in heads:
        lse_ref[h // 2, h % 2 : h % 2 + 1, :] = peaks[h] + jnp.log(totals[h])


def attend(bounds, queries, low, both, turned, g, kv, bq, bk):
    rows, keys = queries.shape[0], both.shape[1]
    cols = queries.shape[1] // kv
    pairs = cols // LANES
    size = rows * cols * keys
    return pl.pallas_call(
        functools.partial(attend_kernel, bq, bk),
        grid_spec=pltpu.PrefetchScalarGridSpec(
            num_scalar_prefetch=1, grid=(rows // bq,),
            in_specs=[
                pl.BlockSpec((bq, cols), lambda i, b: (i, g)),
                pl.BlockSpec((8, bq), lambda i, b: (0, i)),
                pl.BlockSpec((1, keys, LANES), lambda i, b: (g, 0, 0)),
                pl.BlockSpec((HEAD, keys), lambda i, b: (kv + g, 0)),
            ],
            out_specs=[
                pl.BlockSpec((bq, cols), lambda i, b: (i, 0)),
                pl.BlockSpec((pairs, 8, bq), lambda i, b: (0, 0, i)),
            ],
        ),
        out_shape=[
            jax.ShapeDtypeStruct((rows, cols), bf16),
            jax.ShapeDtypeStruct((pairs, 8, rows), f32),
        ],
        compiler_params=pltpu.CompilerParams(vmem_limit_bytes=60 * 2**20),
        cost_estimate=pl.CostEstimate(flops=4 * size, bytes_accessed=8 * rows * cols, transcendentals=size // HEAD),
        name="attend",
    )(bounds, queries, low, both, turned)


def attend_back_kernel(
    bq, bk, pieces, bounds, q_ref, o_ref, low_ref, lse_ref, cos_ref, sin_ref, k_ref, kt_ref, v_ref, *rest
):
    do_refs, (dq_ref, dk_ref, dv_ref, do_rows) = rest[:pieces], rest[pieces:]
    pair, block = pl.program_id(0), pl.program_id(1)

    @pl.when((pair == 0) & (block == 0))
    def _():
        dk_ref[...] = jnp.zeros_like(dk_ref)
        dv_ref[...] = jnp.zeros_like(dv_ref)

    @pl.when(block == 0)
    def _():
        for shift, do_ref in enumerate(do_refs):
            rows = do_ref.shape[0]
            place = lax.rem(bounds[5, 0] + pieces - shift, pieces) * rows
            do_rows[pl.ds(pl.multiple_of(place, rows), rows), :] = do_ref[...]

    do = do_rows[pl.ds(pl.multiple_of(block * bq, bq), bq), :]
    q_of, do_of = halves(q_ref[...]), halves(do)
    product = do.astype(f32) * o_ref[...].astype(f32)
    high = product.astype(bf16)
    low = (product - high.astype(f32)).astype(bf16)
    row = lax.broadcasted_iota(jnp.int32, (8, LANES), 0)
    lane = lax.broadcasted_iota(jnp.int32, (8, LANES), 1)
    ones = jnp.where(lane // HEAD == row, 1.0, 0.0).astype(bf16)
    delta = dot(ones, high, contract_last) + dot(ones, low, contract_last)

    def step(masked, j, accs):
        at = pl.multiple_of(j * bk, bk)
        here = pl.ds(at, bk)
        if masked:
            ok = allowed_keys(at, bounds[0, block], low_ref[:1, :], bk, bq)
        k, v = k_ref[0, here, :], v_ref[0, here, :]
        scores = [dot(k, q_of[h], contract_last) for h in range(2)]
        d_probs = [dot(v, do_of[h], contract_last) for h in range(2)]
        dk, dv, new = [], [], []
        for h in range(2):
            p = jnp.exp(scores[h] - lse_ref[0, h : h + 1, :])
            if masked:
                p = jnp.where(ok, p, 0.0)
            ds = (p * (d_probs[h] - delta[h : h + 1, :])).astype(bf16)
            dv.append(dot(p.astype(bf16), do_of[h]))
            dk.append(dot(ds, q_of[h]))
            new.append(accs[h] + dot(kt_ref[:, here], ds))
        dk_ref[here, :] += dk[0] + dk[1]
        dv_ref[here, :] += dv[0] + dv[1]
        return tuple(new)

    accs = over_blocks(bounds, block, step, (jnp.zeros((HEAD, bq), f32),) * 2)
    g = jnp.concatenate(accs, 0).T
    dq_ref[...] = ((g * cos_ref[...] - swap_halves(g) * sin_ref[...]) * HEAD**-0.5).astype(bf16)


def attend_back(bounds, queries, attended, low, sums, cosine, sine, both, turned, d_attended, g, kv, bq, bk):
    rows, keys = queries.shape[0], both.shape[1]
    cols = queries.shape[1] // kv
    pairs, pieces = cols // LANES, len(d_attended)
    mine = pl.BlockSpec((bq, LANES), lambda p, i, b: (i, p))
    table = pl.BlockSpec((bq, LANES), lambda p, i, b: (i, 0))
    head = lambda at: pl.BlockSpec((1, keys, LANES), lambda p, i, b: (at, 0, 0))
    whole = pl.BlockSpec((keys, LANES), lambda p, i, b: (0, 0))
    size = rows * cols * keys
    return pl.pallas_call(
        functools.partial(attend_back_kernel, bq, bk, pieces),
        grid_spec=pltpu.PrefetchScalarGridSpec(
            num_scalar_prefetch=1, grid=(pairs, rows // bq),
            in_specs=[
                pl.BlockSpec((bq, LANES), lambda p, i, b: (i, g * pairs + p)), mine,
                pl.BlockSpec((8, bq), lambda p, i, b: (0, i)), pl.BlockSpec((1, 8, bq), lambda p, i, b: (p, 0, i)),
                table, table, head(g), pl.BlockSpec((HEAD, keys), lambda p, i, b: (g, 0)), head(kv + g),
            ] + [pl.BlockSpec((rows // pieces, LANES), lambda p, i, b: (0, g * pairs + p))] * pieces,
            out_specs=[mine, whole, whole],
            scratch_shapes=[pltpu.VMEM((rows, LANES), bf16)],
        ),
        out_shape=[jax.ShapeDtypeStruct((rows, cols), bf16)] + [jax.ShapeDtypeStruct((keys, LANES), f32)] * 2,
        compiler_params=pltpu.CompilerParams(vmem_limit_bytes=60 * 2**20),
        cost_estimate=pl.CostEstimate(flops=size, bytes_accessed=8 * rows * cols, transcendentals=size // HEAD),
        name="attend_back",
    )(bounds, queries, attended, low, sums, cosine, sine, both, turned, both, *d_attended)


def block_bounds(starts, low, bq, bk, tp_me):
    low = low.reshape(-1, bq)
    begin, end = low[:, 0] // bk, (starts + bq + bk - 1) // bk
    whole = jnp.clip((low[:, -1] + bk - 1) // bk, begin, end)
    diagonal = jnp.clip((starts + 1) // bk, whole, end)
    return jnp.stack([starts, begin, whole, diagonal, end, jnp.full_like(starts, tp_me)]).astype(jnp.int32)


def ffn_kernel(tiles, earlier, x_ref, c_ref, gate_ref, up_ref, down_ref, *rest):
    act_ref, d_gate_ref, d_up_ref, out_ref, acc = rest[earlier:]
    tile = pl.program_id(0)
    x = x_ref[...]
    c = c_ref[...].reshape(x.shape)
    gate, up = dot(x, gate_ref[...]), dot(x, up_ref[...])
    d_act = dot(c, down_ref[...], contract_last)
    sig = 1.0 / (1.0 + jnp.exp(-gate))
    swish = gate * sig
    d_gate = (d_act * up * sig * (1.0 + gate * (1.0 - sig))).astype(bf16)
    d_up = (d_act * swish).astype(bf16)
    act_ref[...] = (swish * up).astype(bf16).reshape(act_ref.shape)
    d_gate_ref[...] = d_gate.reshape(act_ref.shape)
    d_up_ref[...] = d_up.reshape(act_ref.shape)
    part = dot(d_gate, gate_ref[...], contract_last) + dot(d_up, up_ref[...], contract_last)

    @pl.when(tile == 0)
    def _():
        acc[...] = part

    @pl.when(tile > 0)
    def _():
        acc[...] += part

    @pl.when(tile == tiles - 1)
    def _():
        out_ref[...] = acc[...].astype(bf16)


def ffn_chunk(x, c, gate_weight, up_weight, down_weight, chunk, earlier):
    rows, width = x.shape
    groups, own = c.shape[:2]
    hidden = gate_weight.shape[1]
    tn = min(512, hidden)
    tiles, part = hidden // tn, rows // groups
    column = pl.BlockSpec((width, tn), lambda j: (0, j))
    result = pl.BlockSpec((groups, part, tn), lambda j: (0, chunk, j))
    whole = pl.BlockSpec((rows, width), lambda j: (0, 0))
    return pl.pallas_call(
        functools.partial(ffn_kernel, tiles, len(earlier)),
        grid=(tiles,),
        in_specs=[
            whole, pl.BlockSpec((groups, part, width), lambda j: (0, chunk, 0)), column, column,
            pl.BlockSpec((tn, width), lambda j: (j, 0)),
        ] + [pl.BlockSpec(memory_space=pl.ANY)] * len(earlier),
        out_specs=[result] * 3 + [whole],
        scratch_shapes=[pltpu.VMEM((rows, width), f32)],
        out_shape=[jax.ShapeDtypeStruct((groups, own, hidden), bf16)] * 3
        + [jax.ShapeDtypeStruct((rows, width), bf16)],
        input_output_aliases={5 + i: i for i in range(len(earlier))},
        compiler_params=pltpu.CompilerParams(vmem_limit_bytes=60 * 2**20),
        cost_estimate=pl.CostEstimate(
            flops=16 * rows * width * hidden, bytes_accessed=6 * width * hidden, transcendentals=rows * hidden
        ),
        name="feed_forward",
    )(x, c, gate_weight, up_weight, down_weight, *earlier)


def branch_kernel(shifts, attended_ref, o_ref, x_ref, gain_ref, mid_ref, unit_ref, normed_ref, rstd_ref):
    shift = pl.program_id(0)
    o = o_ref[...].reshape(-1, mid_ref.shape[1])
    groups, wide = attended_ref.shape[1], attended_ref.shape[3]
    part = sum(dot(attended_ref[0, g], o[g * wide : (g + 1) * wide]) for g in range(groups))

    @pl.when(shift == 0)
    def _():
        mid_ref[...] = x_ref[...].astype(f32) + part

    @pl.when(shift > 0)
    def _():
        mid_ref[...] += part

    @pl.when(shift == shifts - 1)
    def _():
        mid = mid_ref[...]
        rstd = lax.rsqrt(jnp.mean(mid * mid, -1, keepdims=True) + epsilon)
        unit = mid * rstd
        unit_ref[...] = unit
        normed_ref[...] = (unit * gain_ref[...]).astype(bf16)
        rstd_ref[...] = jnp.broadcast_to(rstd, rstd_ref.shape)


def branch(attended, o, x, gain):
    shifts, groups, own, wide = attended.shape
    plane, _, rows, width = o.shape
    whole = lambda cols: pl.BlockSpec((own, cols), lambda d: (0, 0))
    shapes = [((own, width), f32), ((own, width), f32), ((own, width), bf16), ((own, LANES), f32)]
    return pl.pallas_call(
        functools.partial(branch_kernel, shifts),
        grid=(shifts,),
        in_specs=[
            pl.BlockSpec((1, groups, own, wide), lambda d: (d, 0, 0, 0)),
            pl.BlockSpec((plane, 1, rows, width), lambda d: (0, d, 0, 0)),
            whole(width), pl.BlockSpec((1, width), lambda d: (0, 0)),
        ],
        out_specs=[whole(shape[1]) for shape, _ in shapes],
        out_shape=[jax.ShapeDtypeStruct(*shape) for shape in shapes],
        compiler_params=pltpu.CompilerParams(vmem_limit_bytes=60 * 2**20),
        name="branch",
    )(attended, o, x, gain[None])


def branch_back_kernel(x_ref, o_ref, out_ref):
    out_ref[0] = dot(x_ref[...], o_ref[...].reshape(-1, x_ref.shape[1]), contract_last).astype(bf16)


def branch_back(x, o):
    plane, shifts, rows, width = o.shape
    own = x.shape[0]
    return pl.pallas_call(
        branch_back_kernel,
        grid=(shifts,),
        in_specs=[
            pl.BlockSpec((own, width), lambda d: (0, 0)),
            pl.BlockSpec((plane, 1, rows, width), lambda d: (0, lax.rem(shifts - d, shifts), 0, 0)),
        ],
        out_specs=pl.BlockSpec((1, own, plane * rows), lambda d: (d, 0, 0)),
        out_shape=jax.ShapeDtypeStruct((shifts, own, plane * rows), bf16),
        compiler_params=pltpu.CompilerParams(vmem_limit_bytes=60 * 2**20),
        name="branch_back",
    )(x, o)


def bits_of(n):
    return [1 << b for b in range(n.bit_length() - 1)]


def exchange(x, axis, bit):
    n = lax.axis_size(axis)
    return lax.ppermute(x, axis, [(i, i ^ bit) for i in range(n)])


def gather_ctx(x):
    n = lax.axis_size("ctx")
    held = {0: x}
    for bit in reversed(bits_of(n)):
        held.update({mask ^ bit: exchange(piece, "ctx", bit) for mask, piece in held.items()})
    return [held[mask] for mask in range(n)]


def scatter_sum_ctx(x):
    n, me = lax.axis_size("ctx"), lax.axis_index("ctx")
    x = x.reshape(n, -1, x.shape[1])
    for bit in bits_of(n):
        x = x.reshape(-1, 2, *x.shape[1:])
        mine = (me // bit) % 2
        send = lax.dynamic_index_in_dim(x, 1 - mine, 1, False)
        keep = lax.dynamic_index_in_dim(x, mine, 1, False)
        x = (keep.astype(f32) + exchange(send, "ctx", bit).astype(f32)).astype(bf16)
    return x[0]


def mirror_ctx(x):
    n = lax.axis_size("ctx")
    return lax.ppermute(x, "ctx", [(i, n - 1 - i) for i in range(n)])


def home_pairs(n_ctx, n_tp, shift):
    pairs = []
    for c in range(n_ctx):
        for t in range(n_tp):
            to = (t + shift) % n_tp
            pairs.append((c * n_tp + t, (c if to < n_tp // 2 else n_ctx - 1 - c) * n_tp + to))
    return pairs


def to_tokens(x):
    n, me = lax.axis_size("tp"), lax.axis_index("tp")
    x = x.reshape(n, -1, x.shape[1])
    out = []
    for d in range(n):
        piece = lax.dynamic_index_in_dim(x, (me + d) % n, 0, False)
        out.append(lax.ppermute(piece, ("ctx", "tp"), home_pairs(lax.axis_size("ctx"), n, d)))
    return out


def to_heads(pieces):
    n, n_ctx = lax.axis_size("tp"), lax.axis_size("ctx")
    out = []
    for d, piece in enumerate(pieces):
        pairs = [(to, at) for at, to in home_pairs(n_ctx, n, (n - d) % n)]
        out.append(lax.ppermute(piece, ("ctx", "tp"), pairs))
    return out


def shift_tp(x, d):
    n = lax.axis_size("tp")
    return lax.ppermute(x, "tp", [(i, (i + d) % n) for i in range(n)]) if d else x


def ring_tp(x):
    n, me = lax.axis_size("tp"), lax.axis_index("tp")
    up, down = [x], [x]
    for step in range(1, n):
        up.append(lax.ppermute(up[-1], "tp", [(i, i + 1) for i in range(step - 1, n - 1)]))
        down.append(lax.ppermute(down[-1], "tp", [(i, i - 1) for i in range(1, n - step + 1)]))
    return [x] + [jnp.where(me >= d, up[d], down[n - d]) for d in range(1, n)]


def in_order(pieces):
    n, me = lax.axis_size("tp"), lax.axis_index("tp")
    pieces = jnp.stack(pieces)
    return jnp.concatenate([lax.dynamic_index_in_dim(pieces, (me - t) % n, 0, False) for t in range(n)], 0)


def scatter_direct(x):
    n, me = lax.axis_size("tp"), lax.axis_index("tp")
    x = x.reshape(n, -1, x.shape[1])
    return sum(shift_tp(lax.dynamic_index_in_dim(x, (me + d) % n, 0, False), d).astype(f32) for d in range(n))


def gather_direct(x):
    return in_order([shift_tp(x, d) for d in range(lax.axis_size("tp"))])


def share_rows(weight):
    plane = lax.axis_size("dp") * lax.axis_size("ctx")
    at = lax.axis_index("dp") * lax.axis_size("ctx") + lax.axis_index("ctx")
    share = lax.dynamic_index_in_dim(weight.reshape(plane, -1, weight.shape[1]), at, 0, False)
    return jnp.concatenate(ring_tp(share), 0)


def gather_shares(shares):
    n = lax.axis_size("tp")
    whole = lax.all_gather(shares, ("dp", "ctx"), axis=0, tiled=True)
    return whole.reshape(-1, n, shares.shape[0] // n, shares.shape[1])


PLANE = ("dp", "ctx")


def sum_plane(*xs):
    return lax.psum(xs, PLANE)


def sum_all(x):
    for axis in ("ctx", "tp", "dp"):
        for bit in bits_of(lax.axis_size(axis)):
            x = x + exchange(x, axis, bit)
    return x


def norm_back(grad, unit, inverse_root, gain):
    scaled = grad * gain
    return inverse_root * (scaled - unit * jnp.mean(scaled * unit, -1, keepdims=True))


def gather_tp(x):
    return lax.all_gather(x, "tp", axis=0, tiled=True)


def scatter_tp(x):
    return lax.psum_scatter(x, "tp", scatter_dimension=0, tiled=True)


def on_device(
    tokens, lengths, q_weight, k_weight, v_weight, o_weight, gate_weight, up_weight, down_weight,
    attention_gain, ffn_gain, cotangent,
):
    ctx, me = lax.axis_size("ctx"), lax.axis_index("ctx")
    own = tokens.shape[1]
    block = own * lax.axis_size("tp")
    half = block // 2
    q_cols, kv_cols = q_weight.shape[1], k_weight.shape[1]
    kv = kv_cols // HEAD

    x = tokens[0].astype(f32)
    rstd1 = lax.rsqrt(jnp.mean(x * x, -1, keepdims=True) + epsilon)
    unit1 = x * rstd1
    pieces = ring_tp((unit1 * attention_gain).astype(bf16))
    o_full = gather_shares(share_rows(o_weight))
    w_kv = jnp.concatenate([k_weight, v_weight], 1)

    index = me * block + jnp.arange(block, dtype=jnp.int32)
    cosine, sine = rope_tables(index - doc_starts(lengths[0], index))
    far = (2 * ctx - 1 - 2 * me) * half
    near = me * block
    steps = jnp.arange(half, dtype=jnp.int32)
    q_index = jnp.concatenate([near + steps, far + steps])
    q_low = doc_starts(lengths[0], q_index)
    q_cos, q_sin = rope_tables(q_index - q_low)
    bq = bk = min(512, half)
    bounds = block_bounds(q_index.reshape(-1, bq)[:, 0], q_low, bq, bk, lax.axis_index("tp"))
    low_rows = jnp.broadcast_to(q_low[None, :], (8, block))
    pieces, w_kv, cosine, sine, q_cos, q_sin, bounds, low_rows = barrier(
        (pieces, w_kv, cosine, sine, q_cos, q_sin, bounds, low_rows)
    )
    here = lax.axis_index("tp")[None]
    kv_own = project(here, pieces, w_kv, cosine, sine, 0, kv_cols)
    kv_all = gather_ctx(kv_own)
    pieces, o_full = barrier((pieces, o_full))
    q_own = project(here, pieces, q_weight, cosine, sine, q_cols, q_cols)
    normed = in_order(pieces)
    queries = jnp.concatenate([q_own[:half], mirror_ctx(q_own[half:])], 0)
    c_own, _ = barrier((cotangent[0], o_full))
    c_full = gather_tp(c_own)
    both, turned = spread(me[None], kv_all, kv)
    parts = [attend(bounds, queries, low_rows, both, turned, g, kv, bq, bk) for g in range(kv)]
    sent = [to_tokens(attended) for attended, _ in parts]
    attended_own = jnp.stack([jnp.stack(pieces) for pieces in zip(*sent)])
    attended_own, c_full = barrier((attended_own, c_full))
    attended_z = jnp.concatenate([attended for attended, _ in parts], 1)
    attended = jnp.concatenate([attended_z[:half], mirror_ctx(attended_z[half:])], 0)

    mid, unit2, ffn_own, rstd2 = branch(attended_own, o_full, tokens[0], ffn_gain)
    rstd2 = rstd2[:, :1]
    part = own // CHUNKS
    tp = lax.axis_size("tp")
    c_rows = c_full.reshape(tp, own, -1)
    gathered, hidden, scattered = [], [], []
    for chunk in range(CHUNKS):
        piece = ffn_own[chunk * part : (chunk + 1) * part]
        if gathered:
            piece, _ = barrier((piece, gathered[-1]))
        gathered.append(gather_tp(piece))
    for chunk in range(CHUNKS):
        *hidden, out = ffn_chunk(gathered[chunk], c_rows, gate_weight, up_weight, down_weight, chunk, hidden)
        scattered.append(scatter_direct(out) if chunk == CHUNKS - 1 else scatter_tp(out).astype(f32))
    act, d_gate, d_up = [h.reshape(block, -1) for h in hidden]
    d_ffn = jnp.concatenate(scattered, 0)
    ffn_normed = jnp.stack([g.reshape(tp, part, -1) for g in gathered], 1).reshape(block, -1)

    d_mid = c_own.astype(f32) + norm_back(d_ffn, unit2, rstd2, ffn_gain)
    ffn_gain_part = jnp.sum(d_ffn * unit2, 0)
    d_gate_w = dot(ffn_normed, d_gate, contract_first).astype(bf16)
    d_up_w = dot(ffn_normed, d_up, contract_first).astype(bf16)
    d_branch, _ = barrier((d_mid.astype(bf16), (d_gate_w, d_up_w)))
    d_gate_w, d_up_w = sum_plane(d_gate_w, d_up_w)
    d_attended = to_heads(list(branch_back(d_branch, o_full)))
    d_branch, d_attended = barrier((d_branch, d_attended))
    d_branch = gather_direct(d_branch)
    d_down = dot(act, c_full, contract_first).astype(bf16)

    act_late, _ = barrier((act, d_branch))
    out_sum = scatter_direct(dot(act_late, down_weight).astype(bf16))

    d_o = dot(attended, d_branch, contract_first).astype(bf16)
    back = [
        attend_back(
            bounds, queries, parts[g][0], low_rows, parts[g][1], q_cos, q_sin, both, turned, d_attended, g, kv, bq, bk
        )
        for g in range(kv)
    ]
    d_q = jnp.concatenate([dq for dq, _, _ in back], 1)
    d_q = jnp.concatenate([d_q[:half], mirror_ctx(d_q[half:])], 0)
    d_kv = jnp.concatenate([back[g][i][:, :HEAD] + back[g][i][:, HEAD:] for i in (1, 2) for g in range(kv)], 1)
    d_kv = rope(scatter_sum_ctx(d_kv.astype(bf16)), cosine, -sine, 0, kv_cols)
    d_normed_part = dot(d_q, q_weight, contract_last) + dot(d_kv, w_kv, contract_last)
    d_normed_part, out_sum = barrier((d_normed_part.astype(bf16), out_sum))
    d_normed = scatter_direct(d_normed_part)
    d_qkv_w = dot(normed, jnp.concatenate([d_q, d_kv], 1), contract_first).astype(bf16)
    d_qkv_w, d_o, d_down, _ = barrier((d_qkv_w, d_o, d_down, (d_gate_w, d_up_w)))
    d_gate_w, d_up_w = d_gate_w.astype(f32), d_up_w.astype(f32)
    d_qkv_w, d_o, d_down = sum_plane(d_qkv_w, d_o, d_down)

    out_sum, _ = barrier((out_sum, (d_gate_w, d_up_w)))
    output = (mid + out_sum).astype(bf16)[None]
    d_normed, _ = barrier((d_normed, output))
    input_gradient = (d_mid + norm_back(d_normed, unit1, rstd1, attention_gain)).astype(bf16)[None]
    attn_gain_part = jnp.sum(d_normed * unit1, 0)
    d_gains = sum_all(jnp.stack([attn_gain_part, ffn_gain_part]))
    d_q_w, d_kv_w = d_qkv_w[:, :q_cols], d_qkv_w[:, q_cols:]
    grads = [
        g.astype(f32)
        for g in (d_q_w, d_kv_w[:, :kv_cols], d_kv_w[:, kv_cols:], d_o)
    ] + [d_gate_w, d_up_w, d_down.astype(f32)]
    return (output, input_gradient, *grads, d_gains[0], d_gains[1])


def solution(mesh):
    rows = P("dp", ("ctx", "tp"), None)
    columns, across = P(None, "tp"), P("tp", None)
    return jax.shard_map(
        on_device,
        mesh=mesh,
        in_specs=(
            rows, P("dp", None), columns, columns, columns, across, columns, columns, across, P(), P(), rows,
        ),
        out_specs=(rows, rows, columns, columns, columns, across, columns, columns, across, P(), P()),
        check_vma=False,
    )
```
